1024 devices in a mesh: seq: 128 (over z, y), head: 8 (over x, core).
Axes of the slice: x: 4, y: 4, z: 32, core: 2. Of those that a mesh axis runs over, the one named last changes fastest.
Arguments:
- queries: bfloat16 [65536, 2048], P(('seq', 'head')), may hold values from -6 to 6
- output_gradient: bfloat16 [65536, 2048], P(('seq', 'head')), may hold values from -6 to 6
- outputs: bfloat16 [65536, 2048], P(('seq', 'head')), may hold values from -6 to 6
- key_vectors: bfloat16 [65536, 1024], P(('seq', 'head')), may hold values from -6 to 6
- values: bfloat16 [65536, 1024], P(('seq', 'head')), may hold values from -6 to 6
- logsum: float32 [16, 65536], P('head', 'seq'), as said below
- pair_list: int32 [500, 3], replicated, may hold values from 0 to 127, as said below
Outputs:
- grad_queries: bfloat16 [65536, 2048], P(('seq', 'head'))
- key_gradient: bfloat16 [65536, 1024], P(('seq', 'head'))
- value_gradient: bfloat16 [65536, 1024], P(('seq', 'head'))
The draws below stay inside these ranges and needn't reach their ends.
Inputs may be any that keep to these rules, and one draw needn't show every extreme that they name: `pair_list`: every block b has the row (b, b, 1). Every other row (a, c, m) has 1 <= a - c <= 4 and m equal to 0 or 2. No pair appears twice; rows come in no particular order. A query block has between 1 and 5 rows, and block 127 has 5. `logsum`: each entry lies between ln(512) + 0.5 and ln(2560) + 0.5.
All inputs are finite; a program needn't handle non-finite values.
Results may differ from the reference program's by a relative error of at most 0.0054.
Values may be sent and summed in bfloat16 or wider, within the bound.
A program may use at most 32 MiB of HBM per device.

```python
import jax
import jax.numpy as jnp
from jax import lax

HEAD_SIZE = 128
KEY_VALUE_HEADS = 8
QUERY_HEADS = 16
BLOCK_TOKENS = 512
WIN = 5
BLOCK_COUNT = 128
SEQUENCE_TOKENS = 65536
PAIRS = 500


def draw_logsum(key, part):
    low_end = jnp.log(jnp.float32(BLOCK_TOKENS)) + 0.5
    spread = jnp.log(jnp.float32(WIN))
    level = jax.random.uniform(jax.random.fold_in(key, 21), (QUERY_HEADS, SEQUENCE_TOKENS), jnp.float32)
    return (low_end + spread * level).astype(jnp.float32)


def draw_pair_list(key, part):
    cand_count = BLOCK_COUNT * (WIN - 1)
    extra = 3 * (BLOCK_COUNT - 4)
    blocks = jnp.repeat(jnp.arange(BLOCK_COUNT, dtype=jnp.int32), WIN - 1)
    offsets = jnp.tile(jnp.arange(1, WIN, dtype=jnp.int32), BLOCK_COUNT)
    valid = blocks - offsets >= 0
    random_bits = jax.random.randint(jax.random.fold_in(key, 11), (cand_count,), 0, 1 << 20)
    ranking = jnp.where(valid, random_bits + 2, 0)
    ranking = jnp.where(blocks == BLOCK_COUNT - 1, (1 << 20) + 2, ranking)
    ranking = ranking * cand_count + jnp.arange(cand_count, dtype=jnp.int32)
    picked = jnp.argsort(-ranking)[:extra]
    kinds = jax.random.randint(jax.random.fold_in(key, 12), (extra,), 0, 2) * 2
    extra_rows = jnp.stack([blocks[picked], blocks[picked] - offsets[picked], kinds], axis=1)
    diag_ids = jnp.arange(BLOCK_COUNT, dtype=jnp.int32)
    diag_rows = jnp.stack([diag_ids, diag_ids, jnp.ones((BLOCK_COUNT,), jnp.int32)], axis=1)
    all_rows = jnp.concatenate([diag_rows, extra_rows], axis=0)
    shuffle = jax.random.permutation(jax.random.fold_in(key, 13), PAIRS)
    return all_rows[shuffle].astype(jnp.int32)


def levels(own_key, extent, shards, smallest, high):
    def one(axis_at, shards_of):
        heights = jax.random.uniform(jax.random.fold_in(jax.random.fold_in(own_key, 6), axis_at), (shards_of,), jnp.float32, smallest / len(shards), high / len(shards))
        return jnp.repeat(jnp.exp(heights), extent[axis_at] // shards_of).reshape((-1,) + (1,) * (len(extent) - axis_at - 1))

    level = one(*shards[0])
    for cut in shards[1:]:
        level = level * one(*cut)
    return level


def noise(stream_key, dims, scale, most, split=(), kind=jnp.bfloat16):
    array = jax.random.normal(stream_key, dims, jnp.float32) * scale
    if len(split) > 0:
        array = levels(stream_key, dims, split, -0.22, 0.18) * array
    return jnp.clip(array, min=-most, max=most).astype(kind)


def setup_inputs(seed: int = 0) -> dict:
    streams_of = jax.random.split(jax.random.key(seed), 8)
    return {
        "queries": noise(streams_of[0], (SEQUENCE_TOKENS, QUERY_HEADS * HEAD_SIZE), 1.0, 6.0, ((0, 1024),)),
        "output_gradient": noise(streams_of[1], (SEQUENCE_TOKENS, QUERY_HEADS * HEAD_SIZE), 1.0, 6.0, ((0, 1024),)),
        "outputs": noise(streams_of[2], (SEQUENCE_TOKENS, QUERY_HEADS * HEAD_SIZE), 1.0, 6.0, ((0, 1024),)),
        "key_vectors": noise(streams_of[3], (SEQUENCE_TOKENS, KEY_VALUE_HEADS * HEAD_SIZE), 1.0, 6.0, ((0, 1024),)),
        "values": noise(streams_of[4], (SEQUENCE_TOKENS, KEY_VALUE_HEADS * HEAD_SIZE), 1.0, 6.0, ((0, 1024),)),
        "logsum": draw_logsum(jax.random.fold_in(streams_of[7], 71), 0),
        "pair_list": draw_pair_list(jax.random.fold_in(streams_of[7], 71), 0),
    }


def block_grads(q_block, do_block, lse_block, delta_block, k_block, v_block, pair_code):
    score_scale = 1.0 / jnp.sqrt(jnp.float32(HEAD_SIZE))
    q_float = q_block.astype(jnp.float32)
    do_float = do_block.astype(jnp.float32)
    k_float = k_block.astype(jnp.float32)
    v_float = v_block.astype(jnp.float32)
    scores = jnp.einsum('qkgd,skd->kgqs', q_float, k_float) * score_scale
    row_ids = jnp.arange(BLOCK_TOKENS)[:, None]
    col_ids = jnp.arange(BLOCK_TOKENS)[None, :]
    allowed = (pair_code == 1) | (pair_code == 2) & (col_ids <= row_ids) | (pair_code == 3) & (col_ids > row_ids)
    probs = jnp.where(allowed, jnp.exp(scores - lse_block[..., None]), jnp.float32(0.0))
    probs_low = probs.astype(jnp.bfloat16).astype(jnp.float32)
    grad_v = jnp.einsum('kgqs,qkgd->skd', probs_low, do_float)
    dprobs = jnp.einsum('qkgd,skd->kgqs', do_float, v_float)
    dscores = (probs * (dprobs - delta_block[..., None]) * score_scale).astype(jnp.bfloat16).astype(jnp.float32)
    grad_q = jnp.einsum('kgqs,skd->qkgd', dscores, k_float)
    grad_k = jnp.einsum('kgqs,qkgd->skd', dscores, q_float)
    return (grad_q, grad_k, grad_v)

def reference(queries, output_gradient, outputs, key_vectors, values, logsum, pair_list):
    group_count = QUERY_HEADS // KEY_VALUE_HEADS
    query_every_row = queries.reshape(BLOCK_COUNT, BLOCK_TOKENS, KEY_VALUE_HEADS, group_count, HEAD_SIZE)
    output_grad_rows = output_gradient.reshape(BLOCK_COUNT, BLOCK_TOKENS, KEY_VALUE_HEADS, group_count, HEAD_SIZE)
    key_every_row = key_vectors.reshape(BLOCK_COUNT, BLOCK_TOKENS, KEY_VALUE_HEADS, HEAD_SIZE)
    value_every_row = values.reshape(BLOCK_COUNT, BLOCK_TOKENS, KEY_VALUE_HEADS, HEAD_SIZE)
    delta_term = lax.optimization_barrier(jnp.sum(output_gradient.astype(jnp.float32).reshape(SEQUENCE_TOKENS, QUERY_HEADS, HEAD_SIZE) * outputs.astype(jnp.float32).reshape(SEQUENCE_TOKENS, QUERY_HEADS, HEAD_SIZE), axis=-1))
    delta_every_row = delta_term.reshape(BLOCK_COUNT, BLOCK_TOKENS, KEY_VALUE_HEADS, group_count).transpose(0, 2, 3, 1)
    logsumexp_rows = logsum.reshape(KEY_VALUE_HEADS, group_count, BLOCK_COUNT, BLOCK_TOKENS).transpose(2, 0, 1, 3)

    def one_pair(carry, pair_row):
        acc_q, key_grad_total, value_grad_total = carry
        q_index = pair_row[0]
        k_index = pair_row[1]
        grad_q, grad_k, grad_v = block_grads(query_every_row[q_index], output_grad_rows[q_index], logsumexp_rows[q_index], delta_every_row[q_index], key_every_row[k_index], value_every_row[k_index], pair_row[2] + 1)
        acc_q = acc_q.at[q_index].add(grad_q)
        key_grad_total = key_grad_total.at[k_index].add(grad_k)
        value_grad_total = value_grad_total.at[k_index].add(grad_v)
        return ((acc_q, key_grad_total, value_grad_total), None)
    start_offset = (jnp.zeros((BLOCK_COUNT, BLOCK_TOKENS, KEY_VALUE_HEADS, group_count, HEAD_SIZE), jnp.float32), jnp.zeros((BLOCK_COUNT, BLOCK_TOKENS, KEY_VALUE_HEADS, HEAD_SIZE), jnp.float32), jnp.zeros((BLOCK_COUNT, BLOCK_TOKENS, KEY_VALUE_HEADS, HEAD_SIZE), jnp.float32))
    (acc_q, key_grad_total, value_grad_total), _ = lax.scan(one_pair, start_offset, pair_list)
    grad_queries = acc_q.reshape(SEQUENCE_TOKENS, QUERY_HEADS * HEAD_SIZE).astype(jnp.bfloat16)
    key_gradient = key_grad_total.reshape(SEQUENCE_TOKENS, KEY_VALUE_HEADS * HEAD_SIZE).astype(jnp.bfloat16)
    value_gradient = value_grad_total.reshape(SEQUENCE_TOKENS, KEY_VALUE_HEADS * HEAD_SIZE).astype(jnp.bfloat16)
    return (grad_queries, key_gradient, value_gradient)
```

```python
import jax
import jax.numpy as jnp
from jax import lax
from jax.experimental import pallas as pl
from jax.experimental.pallas import tpu as pltpu
from jax.sharding import PartitionSpec as P

D = 128
BLK = 512
TOK = 64
HEADS = 8
SEQ = 128
WIN = 5
LOG2E = 1.4426950408889634
SCALE = 1.0 / D**0.5
BIG = 1e30
F32 = jnp.float32
BF16 = jnp.bfloat16
MESH = pl.DeviceIdType.MESH
PEER_ORDER = (4, 3, 5, 2, 6, 1, 7)


def dot_nt(a, b):
    return lax.dot_general(a, b, (((1,), (1,)), ((), ())), preferred_element_type=F32)


def dot_nn(a, b):
    return lax.dot_general(a, b, (((1,), (0,)), ((), ())), preferred_element_type=F32)


def wait_bytes(ref, sem):
    pltpu.make_async_copy(ref, ref, sem).wait()


def kernel(
    q_hbm, do_hbm, o_hbm, k_hbm, v_hbm, lse_hbm, pairs_hbm,
    oq_ref, ok_ref, ov_ref,
    kv, qs, dos, do_own, o_own, lse, pairs, dls, dlr, accq, own_g, gsend, grecv, fin_q, fin_kv,
    loc_sem, in_recv, in_send, kv_recv, kv_send, g_recv, g_send, out_recv, out_send,
):
    s = lax.axis_index("seq")
    h = lax.axis_index("head")

    c_do = pltpu.make_async_copy(do_hbm, do_own, loc_sem.at[0])
    c_o = pltpu.make_async_copy(o_hbm, o_own, loc_sem.at[1])
    c_lse = pltpu.make_async_copy(lse_hbm, lse, loc_sem.at[2])
    c_pairs = pltpu.make_async_copy(pairs_hbm, pairs, loc_sem.at[3])
    for c in (c_do, c_o, c_lse, c_pairs):
        c.start()

    barrier = pltpu.get_barrier_semaphore()
    for j in range(1, HEADS):
        pl.semaphore_signal(barrier, inc=1, device_id=(s, lax.rem(h + j, HEADS)), device_id_type=MESH)
    for j in range(1, WIN):
        pl.semaphore_signal(barrier, inc=1, device_id=(lax.rem(s + j, SEQ), h), device_id_type=MESH)
        pl.semaphore_signal(
            barrier, inc=1, device_id=(lax.rem(s + SEQ - j, SEQ), h), device_id_type=MESH
        )
    pl.semaphore_wait(barrier, HEADS - 1 + 2 * (WIN - 1))

    my_rows = pl.ds(pl.multiple_of(h * TOK, TOK), TOK)

    def cols(p, width):
        return pl.ds(pl.multiple_of(p * width, width), width)

    def spread(src, dst, width, n):
        for j in PEER_ORDER:
            p = lax.rem(h + j, HEADS)
            pltpu.make_async_remote_copy(
                src_ref=src.at[:, cols(p, width)],
                dst_ref=dst,
                send_sem=in_send.at[n],
                recv_sem=in_recv.at[0 if n < 2 else n - 1],
                device_id=(s, p),
                device_id_type=MESH,
            ).start()
        pltpu.make_async_copy(
            src.at[:, cols(h, width)], dst, in_recv.at[0 if n < 2 else n - 1]
        ).start()

    spread(k_hbm, kv.at[0, my_rows, 0:D], D, 0)
    spread(v_hbm, kv.at[0, my_rows, D : 2 * D], D, 1)
    spread(q_hbm, qs.at[my_rows, :], 2 * D, 2)
    spread(do_hbm, dos.at[my_rows, :], 2 * D, 3)

    c_do.wait()
    c_o.wait()
    row8 = lax.broadcasted_iota(jnp.int32, (8, 2 * D), 0)
    col8 = lax.broadcasted_iota(jnp.int32, (8, 2 * D), 1)
    select = jnp.where((col8 >= row8 * D) & (col8 < row8 * D + D), 1.0, 0.0).astype(BF16)
    lane = lax.broadcasted_iota(jnp.int32, (8, D), 1)
    low = lax.rem(h, 2) * TOK
    mine = jnp.where((lane >= low) & (lane < low + TOK), 1.0, 0.0)
    for p in range(HEADS):
        c = slice(p * 2 * D, (p + 1) * 2 * D)
        prod = do_own[:, c].astype(F32) * o_own[:, c].astype(F32)
        prod = jnp.concatenate([prod, prod], axis=0)
        hi = prod.astype(BF16)
        mid = (prod - hi.astype(F32)).astype(BF16)
        dls[p] = (dot_nt(select, hi) + dot_nt(select, mid)) * mine
    for j in PEER_ORDER:
        p = lax.rem(h + j, HEADS)
        pltpu.make_async_remote_copy(
            src_ref=dls.at[p],
            dst_ref=dlr.at[h],
            send_sem=in_send.at[4],
            recv_sem=in_recv.at[3],
            device_id=(s, p),
            device_id_type=MESH,
        ).start()
    pltpu.make_async_copy(dls.at[h], dlr.at[h], in_recv.at[3]).start()

    wait_bytes(kv.at[0], in_recv.at[0])
    for d in (2, 4, 3, 1):
        pltpu.make_async_remote_copy(
            src_ref=kv.at[0],
            dst_ref=kv.at[d],
            send_sem=kv_send,
            recv_sem=kv_recv.at[d],
            device_id=(lax.rem(s + d, SEQ), h),
            device_id_type=MESH,
        ).start()

    c_lse.wait()
    c_pairs.wait()
    pa = pairs[0:1, :]
    pc = pairs[1:2, :]
    pm = pairs[2:3, :]
    accq[...] = jnp.zeros_like(accq)

    wait_bytes(qs, in_recv.at[1])
    wait_bytes(dos, in_recv.at[2])
    wait_bytes(dlr, in_recv.at[3])
    delta = jnp.concatenate([dlr[2 * i] + dlr[2 * i + 1] for i in range(HEADS // 2)], axis=1)
    lse2 = lse[...] * LOG2E

    def pair_step(pd, carry):
        d = lax.rem(3 * pd, WIN)

        @pl.when(pd > 0)
        def _():
            wait_bytes(kv.at[d], kv_recv.at[d])

        match = (pa == s) & (pc == s - d)
        code = jnp.max(jnp.where(match, pm + 1, 0), axis=1, keepdims=True)
        lo = jnp.where((code == 1) | (code == 2), -BLK, jnp.where(code == 3, 0, BLK))
        hi = jnp.where(code == 2, 1, BLK)
        diff = lax.broadcasted_iota(jnp.int32, (BLK, BLK), 0) - lax.broadcasted_iota(
            jnp.int32, (BLK, BLK), 1
        )
        bias = jnp.where((diff > lo) & (diff < hi), 0.0, BIG).astype(F32)
        k = kv[d, :, 0:D]
        v = kv[d, :, D : 2 * D]
        kt = k.T
        gk = jnp.zeros((BLK, D), F32)
        gv = jnp.zeros((BLK, D), F32)
        for g in range(2):
            c = slice(g * D, (g + 1) * D)
            q = qs[:, c]
            do = dos[:, c]
            prob = jnp.exp2(dot_nt(k, q) * (SCALE * LOG2E) - lse2[g : g + 1, :] - bias)
            ds = (prob * (dot_nt(v, do) - delta[g : g + 1, :])).astype(BF16)
            gv = gv + dot_nn(prob.astype(BF16), do)
            gk = gk + dot_nn(ds, q)
            accq[c, :] += dot_nn(kt, ds)

        @pl.when(pd == 0)
        def _():
            own_g[:, 0:D] = gk
            own_g[:, D : 2 * D] = gv

        @pl.when(pd > 0)
        def _():
            gsend[d, :, 0:D] = gk.astype(BF16)
            gsend[d, :, D : 2 * D] = gv.astype(BF16)
            pltpu.make_async_remote_copy(
                src_ref=gsend.at[d],
                dst_ref=grecv.at[d],
                send_sem=g_send,
                recv_sem=g_recv.at[d],
                device_id=(lax.rem(s + SEQ - d, SEQ), h),
                device_id_type=MESH,
            ).start()

        return carry

    lax.fori_loop(0, WIN, pair_step, 0)

    def gather(src, col, width, dst, n):
        for j in PEER_ORDER:
            p = lax.rem(h + j, HEADS)
            pltpu.make_async_remote_copy(
                src_ref=src.at[cols(p, TOK), col],
                dst_ref=dst.at[:, cols(h, width)],
                send_sem=out_send.at[n],
                recv_sem=out_recv.at[n],
                device_id=(s, p),
                device_id_type=MESH,
            ).start()
        pltpu.make_async_copy(
            src.at[my_rows, col], dst.at[:, cols(h, width)], out_recv.at[n]
        ).start()

    for g in range(2):
        c = slice(g * D, (g + 1) * D)
        fin_q[:, c] = (accq[c, :] * SCALE).T.astype(BF16)
    gather(fin_q, slice(0, 2 * D), 2 * D, oq_ref, 0)

    for d in range(1, WIN):
        wait_bytes(grecv.at[d], g_recv.at[d])
    tot = own_g[...]
    for d in range(1, WIN):
        tot = tot + grecv[d].astype(F32)
    fin_kv[:, 0:D] = (tot[:, 0:D] * SCALE).astype(BF16)
    fin_kv[:, D : 2 * D] = tot[:, D : 2 * D].astype(BF16)
    gather(fin_kv, slice(0, D), D, ok_ref, 1)
    gather(fin_kv, slice(D, 2 * D), D, ov_ref, 2)

    most = (HEADS - 1) * TOK
    wait_bytes(kv.at[0, 0:most, 0:D], in_send.at[0])
    wait_bytes(kv.at[0, 0:most, 0:D], in_send.at[1])
    wait_bytes(qs.at[0:most], in_send.at[2])
    wait_bytes(qs.at[0:most], in_send.at[3])
    wait_bytes(dlr.at[0 : HEADS - 1], in_send.at[4])
    wait_bytes(kv.at[1:WIN], kv_send)
    wait_bytes(gsend.at[1:WIN], g_send)
    wait_bytes(fin_q.at[0:most], out_send.at[0])
    wait_bytes(fin_kv.at[0:most, 0:D], out_send.at[1])
    wait_bytes(fin_kv.at[0:most, 0:D], out_send.at[2])
    wait_bytes(oq_ref, out_recv.at[0])
    wait_bytes(ok_ref, out_recv.at[1])
    wait_bytes(ov_ref, out_recv.at[2])


def shards(queries, output_gradient, outputs, key_vectors, values, logsum, pair_list):
    any_spec = pl.BlockSpec(memory_space=pl.ANY)
    return pl.pallas_call(
        kernel,
        out_shape=(
            jax.ShapeDtypeStruct((TOK, 2 * D * HEADS), BF16),
            jax.ShapeDtypeStruct((TOK, D * HEADS), BF16),
            jax.ShapeDtypeStruct((TOK, D * HEADS), BF16),
        ),
        in_specs=[any_spec] * 7,
        out_specs=(any_spec,) * 3,
        scratch_shapes=[
            pltpu.VMEM((WIN, BLK, 2 * D), BF16),
            pltpu.VMEM((BLK, 2 * D), BF16),
            pltpu.VMEM((BLK, 2 * D), BF16),
            pltpu.VMEM((TOK, 2 * D * HEADS), BF16),
            pltpu.VMEM((TOK, 2 * D * HEADS), BF16),
            pltpu.VMEM((2, BLK), F32),
            pltpu.VMEM((3, 500), jnp.int32),
            pltpu.VMEM((HEADS, 8, D), F32),
            pltpu.VMEM((HEADS, 8, D), F32),
            pltpu.VMEM((2 * D, BLK), F32),
            pltpu.VMEM((BLK, 2 * D), F32),
            pltpu.VMEM((WIN, BLK, 2 * D), BF16),
            pltpu.VMEM((WIN, BLK, 2 * D), BF16),
            pltpu.VMEM((BLK, 2 * D), BF16),
            pltpu.VMEM((BLK, 2 * D), BF16),
            pltpu.SemaphoreType.DMA((4,)),
            pltpu.SemaphoreType.DMA((4,)),
            pltpu.SemaphoreType.DMA((5,)),
            pltpu.SemaphoreType.DMA((WIN,)),
            pltpu.SemaphoreType.DMA,
            pltpu.SemaphoreType.DMA((WIN,)),
            pltpu.SemaphoreType.DMA,
            pltpu.SemaphoreType.DMA((3,)),
            pltpu.SemaphoreType.DMA((3,)),
        ],
        compiler_params=pltpu.CompilerParams(
            collective_id=0, has_side_effects=True, vmem_limit_bytes=60 * 2**20
        ),
        cost_estimate=pl.CostEstimate(
            flops=2 * WIN * 2 * 5 * BLK * BLK * D,
            bytes_accessed=3 * 2**19,
            transcendentals=WIN * 2 * BLK * BLK,
        ),
    )(
        queries, output_gradient, outputs, key_vectors, values, logsum, jnp.transpose(pair_list)
    )


def solution(mesh):
    tok = P(("seq", "head"), None)
    return jax.shard_map(
        shards,
        mesh=mesh,
        in_specs=(tok, tok, tok, tok, tok, P("head", "seq"), P()),
        out_specs=(tok, tok, tok),
        check_vma=False,
    )
```

```python
import jax
import jax.numpy as jnp
from jax import lax
from jax.experimental import pallas as pl
from jax.experimental.pallas import tpu as pltpu
from jax.sharding import PartitionSpec as P

D = 128
BLK = 512
TOK = 64
HEADS = 8
PLANE = 4
DEPTH = 32
WIN = 5
CHUNKS = 4
CROWS = BLK // CHUNKS
HALF = BLK // 2
LOG2E = 1.4426950408889634
SCALE = 1.0 / D**0.5
BIG = 1e30
F32 = jnp.float32
BF16 = jnp.bfloat16
MESH = pl.DeviceIdType.MESH
PEER_ORDER = (4, 3, 5, 2, 6, 1, 7)


def dot_nt(a, b):
    return lax.dot_general(a, b, (((1,), (1,)), ((), ())), preferred_element_type=F32)


def dot_nn(a, b):
    return lax.dot_general(a, b, (((1,), (0,)), ((), ())), preferred_element_type=F32)


def wait_bytes(ref, sem):
    pltpu.make_async_copy(ref, ref, sem).wait()


def kernel(
    q_hbm, do_hbm, o_hbm, k_hbm, v_hbm, lse_hbm, pairs_hbm,
    oq_ref, ok_ref, ov_ref,
    kv, qs, dos, do_own, o_own, lse, pairs, dls, dlr, accq, own_g, gsend, grecv, fin_q, fin_kv,
    loc_sem, in_recv, in_send, kvz_recv, kvz_send, kv_recv, kv_send, g_recv, g_send, out_recv, out_send,
):
    s = lax.axis_index("seq")
    h = lax.axis_index("head")

    c_do = pltpu.make_async_copy(do_hbm, do_own, loc_sem.at[0])
    c_o = pltpu.make_async_copy(o_hbm, o_own, loc_sem.at[1])
    c_lse = pltpu.make_async_copy(lse_hbm, lse, loc_sem.at[2])
    c_pairs = pltpu.make_async_copy(pairs_hbm, pairs, loc_sem.at[3])
    for c in (c_do, c_o, c_lse, c_pairs):
        c.start()

    z = s // PLANE
    y = lax.rem(s, PLANE)

    def in_plane(step):
        return z * PLANE + lax.rem(y + step, PLANE)

    up = lax.rem(s + PLANE, PLANE * DEPTH)
    down = lax.rem(s + PLANE * (DEPTH - 1), PLANE * DEPTH)

    above = (z + DEPTH - 1) // DEPTH
    below = (2 * DEPTH - 2 - z) // DEPTH
    barrier = pltpu.get_barrier_semaphore()
    for j in range(1, HEADS):
        pl.semaphore_signal(barrier, inc=1, device_id=(s, lax.rem(h + j, HEADS)), device_id_type=MESH)
    for d in range(1, PLANE):

        @pl.when((d <= y) | (z > 0))
        def _():
            pl.semaphore_signal(
                barrier, inc=1, device_id=(in_plane(PLANE - d), h), device_id_type=MESH
            )

    @pl.when(z > 0)
    def _():
        pl.semaphore_signal(barrier, inc=1, device_id=(down, h), device_id_type=MESH)

    pl.semaphore_wait(barrier, HEADS - 1 + (PLANE - 1 - y) + above * y + below)

    my_rows = pl.ds(pl.multiple_of(h * TOK, TOK), TOK)

    def cols(p, width):
        return pl.ds(pl.multiple_of(p * width, width), width)

    def spread(src, dst, width, n):
        for j in PEER_ORDER:
            p = lax.rem(h + j, HEADS)
            pltpu.make_async_remote_copy(
                src_ref=src.at[:, cols(p, width)],
                dst_ref=dst,
                send_sem=in_send.at[n],
                recv_sem=in_recv.at[0 if n < 2 else n - 1],
                device_id=(s, p),
                device_id_type=MESH,
            ).start()
        pltpu.make_async_copy(
            src.at[:, cols(h, width)], dst, in_recv.at[0 if n < 2 else n - 1]
        ).start()

    spread(k_hbm, kv.at[0, my_rows, 0:D], D, 0)
    spread(v_hbm, kv.at[0, my_rows, D : 2 * D], D, 1)
    spread(q_hbm, qs.at[my_rows, :], 2 * D, 2)
    spread(do_hbm, dos.at[my_rows, :], 2 * D, 3)

    c_do.wait()
    c_o.wait()
    row8 = lax.broadcasted_iota(jnp.int32, (8, 2 * D), 0)
    col8 = lax.broadcasted_iota(jnp.int32, (8, 2 * D), 1)
    select = jnp.where((col8 >= row8 * D) & (col8 < row8 * D + D), 1.0, 0.0).astype(BF16)
    lane = lax.broadcasted_iota(jnp.int32, (8, D), 1)
    low = lax.rem(h, 2) * TOK
    mine = jnp.where((lane >= low) & (lane < low + TOK), 1.0, 0.0)
    for p in range(HEADS):
        c = slice(p * 2 * D, (p + 1) * 2 * D)
        prod = do_own[:, c].astype(F32) * o_own[:, c].astype(F32)
        prod = jnp.concatenate([prod, prod], axis=0)
        hi = prod.astype(BF16)
        mid = (prod - hi.astype(F32)).astype(BF16)
        dls[p] = (dot_nt(select, hi) + dot_nt(select, mid)) * mine
    for j in PEER_ORDER:
        p = lax.rem(h + j, HEADS)
        pltpu.make_async_remote_copy(
            src_ref=dls.at[p],
            dst_ref=dlr.at[h],
            send_sem=in_send.at[4],
            recv_sem=in_recv.at[3],
            device_id=(s, p),
            device_id_type=MESH,
        ).start()
    pltpu.make_async_copy(dls.at[h], dlr.at[h], in_recv.at[3]).start()

    wait_bytes(kv.at[0], in_recv.at[0])

    def kv_in_plane(d, slot, rows, half):
        pltpu.make_async_remote_copy(
            src_ref=kv.at[slot, rows],
            dst_ref=kv.at[d, rows],
            send_sem=kv_send.at[2 * d + half],
            recv_sem=kv_recv.at[2 * d + half],
            device_id=(in_plane(d), h),
            device_id_type=MESH,
        ).start()

    for half in range(2):

        @pl.when(z < DEPTH - 1)
        def _():
            for i in range(half * CHUNKS // 2, (half + 1) * CHUNKS // 2):
                rows = slice(i * CROWS, (i + 1) * CROWS)
                pltpu.make_async_remote_copy(
                    src_ref=kv.at[0, rows],
                    dst_ref=kv.at[4, rows],
                    send_sem=kvz_send.at[i],
                    recv_sem=kvz_recv.at[i],
                    device_id=(up, h),
                    device_id_type=MESH,
                ).start()

        for d in (2, 3, 1):

            @pl.when(y + d < PLANE)
            def _():
                kv_in_plane(d, 0, slice(half * HALF, (half + 1) * HALF), half)

    @pl.when((z > 0) & (y > 0))
    def _():
        for i in range(CHUNKS):
            rows = slice(i * CROWS, (i + 1) * CROWS)
            wait_bytes(kv.at[4, rows], kvz_recv.at[i])
            for d in (2, 3, 1):

                @pl.when(y + d >= PLANE)
                def _():
                    kv_in_plane(d, 4, rows, 2 * i // CHUNKS)

    c_lse.wait()
    c_pairs.wait()
    pa = pairs[0:1, :]
    pc = pairs[1:2, :]
    pm = pairs[2:3, :]
    accq[...] = jnp.zeros_like(accq)

    wait_bytes(qs, in_recv.at[1])
    wait_bytes(dos, in_recv.at[2])
    wait_bytes(dlr, in_recv.at[3])
    delta = jnp.concatenate([dlr[2 * i] + dlr[2 * i + 1] for i in range(HEADS // 2)], axis=1)
    lse2 = lse[...] * LOG2E

    def pair_step(t, carry):
        late = t // 8
        d = late * 4 + (1 - late) * lax.rem(t, 4)
        half = late * lax.rem(t, 4) + (1 - late) * (t // 4)

        @pl.when((z > 0) | (d <= y))
        def _():
            half_pair(d, half)

        return carry

    def half_pair(d, half):
        rows = pl.ds(pl.multiple_of(half * HALF, HALF), HALF)

        @pl.when((d > 0) & (d < 4))
        def _():
            wait_bytes(kv.at[d, rows], kv_recv.at[2 * d + half])

        @pl.when((d == 4) & (y == 0))
        def _():
            for i in range(CHUNKS // 2):
                wait_bytes(kv.at[4, 0:CROWS], kvz_recv.at[half * (CHUNKS // 2) + i])

        match = (pa == s) & (pc == s - d)
        code = jnp.max(jnp.where(match, pm + 1, 0), axis=1, keepdims=True)
        lo = jnp.where((code == 1) | (code == 2), -BLK, jnp.where(code == 3, 0, BLK))
        hi = jnp.where(code == 2, 1, BLK)
        diff = (
            lax.broadcasted_iota(jnp.int32, (HALF, BLK), 0)
            + half * HALF
            - lax.broadcasted_iota(jnp.int32, (HALF, BLK), 1)
        )
        bias = jnp.where((diff > lo) & (diff < hi), 0.0, BIG).astype(F32)
        k = kv[d, rows, 0:D]
        v = kv[d, rows, D : 2 * D]
        kt = k.T
        gk = jnp.zeros((HALF, D), F32)
        gv = jnp.zeros((HALF, D), F32)
        for g in range(2):
            c = slice(g * D, (g + 1) * D)
            q = qs[:, c]
            do = dos[:, c]
            prob = jnp.exp2(dot_nt(k, q) * (SCALE * LOG2E) - lse2[g : g + 1, :] - bias)
            ds = (prob * (dot_nt(v, do) - delta[g : g + 1, :])).astype(BF16)
            gv = gv + dot_nn(prob.astype(BF16), do)
            gk = gk + dot_nn(ds, q)
            accq[c, :] += dot_nn(kt, ds)

        keep = (d == 0) | (d == 4)

        @pl.when(keep)
        def _():
            own_g[d // 4, rows, 0:D] = gk
            own_g[d // 4, rows, D : 2 * D] = gv

        @pl.when(jnp.logical_not(keep))
        def _():
            gsend[d, rows, 0:D] = gk.astype(BF16)
            gsend[d, rows, D : 2 * D] = gv.astype(BF16)
            pltpu.make_async_remote_copy(
                src_ref=gsend.at[d, rows],
                dst_ref=grecv.at[d, rows],
                send_sem=g_send.at[2 * d + half],
                recv_sem=g_recv.at[2 * d + half],
                device_id=(in_plane(PLANE - d), h),
                device_id_type=MESH,
            ).start()

    lax.fori_loop(0, 2 * WIN, pair_step, 0)

    def gather(src, col, width, dst, n, half):
        for j in range(HEADS // 2):
            p = half * (HEADS // 2) + lax.rem(h + j, HEADS // 2)

            @pl.when(p != h)
            def _():
                pltpu.make_async_remote_copy(
                    src_ref=src.at[cols(p, TOK), col],
                    dst_ref=dst.at[:, cols(h, width)],
                    send_sem=out_send.at[n],
                    recv_sem=out_recv.at[n],
                    device_id=(s, p),
                    device_id_type=MESH,
                ).start()

            @pl.when(p == h)
            def _():
                pltpu.make_async_copy(
                    src.at[my_rows, col], dst.at[:, cols(h, width)], out_recv.at[n]
                ).start()

    halves = (slice(0, HALF), slice(HALF, BLK))

    def to_plane_before(i):
        @pl.when(z > 0)
        def _():
            for d in (1, 2, 3):

                @pl.when(y + d >= PLANE)
                def _():
                    wait_bytes(grecv.at[d, halves[i]], g_recv.at[2 * d + i])
                    own_g[1, halves[i]] += grecv[d, halves[i]].astype(F32)

            gsend[0, halves[i]] = own_g[1, halves[i]].astype(BF16)
            pltpu.make_async_remote_copy(
                src_ref=gsend.at[0, halves[i]],
                dst_ref=grecv.at[0, halves[i]],
                send_sem=g_send.at[i],
                recv_sem=g_recv.at[i],
                device_id=(down, h),
                device_id_type=MESH,
            ).start()

    to_plane_before(0)
    for g in range(2):
        c = slice(g * D, (g + 1) * D)
        fin_q[:, c] = (accq[c, :] * SCALE).T.astype(BF16)
    for half in range(2):
        gather(fin_q, slice(0, 2 * D), 2 * D, oq_ref, 0, half)
    to_plane_before(1)

    for i in range(2):
        for d in (1, 2, 3):

            @pl.when(y + d < PLANE)
            def _():
                wait_bytes(grecv.at[d, halves[i]], g_recv.at[2 * d + i])
                own_g[0, halves[i]] += grecv[d, halves[i]].astype(F32)

        @pl.when(z < DEPTH - 1)
        def _():
            wait_bytes(grecv.at[0, halves[i]], g_recv.at[i])
            own_g[0, halves[i]] += grecv[0, halves[i]].astype(F32)

        fin_kv[halves[i], 0:D] = (own_g[0, halves[i], 0:D] * SCALE).astype(BF16)
        fin_kv[halves[i], D : 2 * D] = own_g[0, halves[i], D : 2 * D].astype(BF16)
        gather(fin_kv, slice(0, D), D, ok_ref, 1, i)
        gather(fin_kv, slice(D, 2 * D), D, ov_ref, 2, i)

    most = (HEADS - 1) * TOK
    wait_bytes(kv.at[0, 0:most, 0:D], in_send.at[0])
    wait_bytes(kv.at[0, 0:most, 0:D], in_send.at[1])
    wait_bytes(qs.at[0:most], in_send.at[2])
    wait_bytes(qs.at[0:most], in_send.at[3])
    wait_bytes(dlr.at[0 : HEADS - 1], in_send.at[4])

    @pl.when(z < DEPTH - 1)
    def _():
        for i in range(CHUNKS):
            wait_bytes(kv.at[0, 0:CROWS], kvz_send.at[i])

    for i in range(2):

        @pl.when(z > 0)
        def _():
            wait_bytes(gsend.at[0, halves[i]], g_send.at[i])

        for d in range(1, PLANE):

            @pl.when((y + d < PLANE) | (z > 0))
            def _():
                wait_bytes(kv.at[d, halves[i]], kv_send.at[2 * d + i])

            @pl.when((d <= y) | (z > 0))
            def _():
                wait_bytes(gsend.at[d, halves[i]], g_send.at[2 * d + i])

    wait_bytes(fin_q.at[0:most], out_send.at[0])
    wait_bytes(fin_kv.at[0:most, 0:D], out_send.at[1])
    wait_bytes(fin_kv.at[0:most, 0:D], out_send.at[2])
    wait_bytes(oq_ref, out_recv.at[0])
    wait_bytes(ok_ref, out_recv.at[1])
    wait_bytes(ov_ref, out_recv.at[2])


def hand_on(q_ref, k_ref, v_ref, oq_ref, ok_ref, ov_ref, q_buf, k_buf, v_buf, sem_in, sem_out):
    buffers = ((q_ref, q_buf, oq_ref), (k_ref, k_buf, ok_ref), (v_ref, v_buf, ov_ref))
    arrive = [
        pltpu.make_async_copy(src, buf, sem_in.at[n]) for n, (src, buf, dst) in enumerate(buffers)
    ]
    leave = [
        pltpu.make_async_copy(buf, dst, sem_out.at[n]) for n, (src, buf, dst) in enumerate(buffers)
    ]
    for c in arrive:
        c.start()
    for a, b in zip(arrive, leave):
        a.wait()
        b.start()
    for c in leave:
        c.wait()


def shards(queries, output_gradient, outputs, key_vectors, values, logsum, pair_list):
    any_spec = pl.BlockSpec(memory_space=pl.ANY)
    out_shape = (
        jax.ShapeDtypeStruct((TOK, 2 * D * HEADS), BF16),
        jax.ShapeDtypeStruct((TOK, D * HEADS), BF16),
        jax.ShapeDtypeStruct((TOK, D * HEADS), BF16),
    )
    grads = pl.pallas_call(
        kernel,
        out_shape=out_shape,
        in_specs=[any_spec] * 7,
        out_specs=(any_spec,) * 3,
        scratch_shapes=[
            pltpu.VMEM((WIN, BLK, 2 * D), BF16),
            pltpu.VMEM((BLK, 2 * D), BF16),
            pltpu.VMEM((BLK, 2 * D), BF16),
            pltpu.VMEM((TOK, 2 * D * HEADS), BF16),
            pltpu.VMEM((TOK, 2 * D * HEADS), BF16),
            pltpu.VMEM((2, BLK), F32),
            pltpu.VMEM((3, 500), jnp.int32),
            pltpu.VMEM((HEADS, 8, D), F32),
            pltpu.VMEM((HEADS, 8, D), F32),
            pltpu.VMEM((2 * D, BLK), F32),
            pltpu.VMEM((2, BLK, 2 * D), F32),
            pltpu.VMEM((PLANE, BLK, 2 * D), BF16),
            pltpu.VMEM((PLANE, BLK, 2 * D), BF16),
            pltpu.VMEM((BLK, 2 * D), BF16),
            pltpu.VMEM((BLK, 2 * D), BF16),
            pltpu.SemaphoreType.DMA((4,)),
            pltpu.SemaphoreType.DMA((4,)),
            pltpu.SemaphoreType.DMA((5,)),
            pltpu.SemaphoreType.DMA((CHUNKS,)),
            pltpu.SemaphoreType.DMA((CHUNKS,)),
            pltpu.SemaphoreType.DMA((2 * PLANE,)),
            pltpu.SemaphoreType.DMA((2 * PLANE,)),
            pltpu.SemaphoreType.DMA((2 * PLANE,)),
            pltpu.SemaphoreType.DMA((2 * PLANE,)),
            pltpu.SemaphoreType.DMA((3,)),
            pltpu.SemaphoreType.DMA((3,)),
        ],
        compiler_params=pltpu.CompilerParams(
            collective_id=0, has_side_effects=True, vmem_limit_bytes=60 * 2**20
        ),
        cost_estimate=pl.CostEstimate(
            flops=2 * WIN * 2 * 5 * BLK * BLK * D,
            bytes_accessed=3 * 2**19,
            transcendentals=WIN * 2 * BLK * BLK,
        ),
    )(
        queries, output_gradient, outputs, key_vectors, values, logsum, jnp.transpose(pair_list)
    )
    return pl.pallas_call(
        hand_on,
        out_shape=out_shape,
        in_specs=[any_spec] * 3,
        out_specs=(any_spec,) * 3,
        scratch_shapes=[pltpu.VMEM(o.shape, o.dtype) for o in out_shape]
        + [pltpu.SemaphoreType.DMA((3,)), pltpu.SemaphoreType.DMA((3,))],
        compiler_params=pltpu.CompilerParams(vmem_limit_bytes=60 * 2**20),
    )(*grads)


def solution(mesh):
    tok = P(("seq", "head"), None)
    return jax.shard_map(
        shards,
        mesh=mesh,
        in_specs=(tok, tok, tok, tok, tok, P("head", "seq"), P()),
        out_specs=(tok, tok, tok),
        check_vma=False,
    )
```

```python
import jax
import jax.numpy as jnp
from jax import lax
from jax.experimental import pallas as pl
from jax.experimental.pallas import tpu as pltpu
from jax.sharding import PartitionSpec as P

D = 128
BLK = 512
TOK = 64
HEADS = 8
PLANE = 4
DEPTH = 32
WIN = 5
CHUNKS = 4
CROWS = BLK // CHUNKS
HALF = BLK // 2
LOG2E = 1.4426950408889634
SCALE = 1.0 / D**0.5
BIG = 1e30
F32 = jnp.float32
BF16 = jnp.bfloat16
MESH = pl.DeviceIdType.MESH
PEER_ORDER = (4, 3, 5, 2, 6, 1, 7)


def dot_nt(a, b):
    return lax.dot_general(a, b, (((1,), (1,)), ((), ())), preferred_element_type=F32)


def dot_nn(a, b):
    return lax.dot_general(a, b, (((1,), (0,)), ((), ())), preferred_element_type=F32)


def wait_bytes(ref, sem):
    pltpu.make_async_copy(ref, ref, sem).wait()


def kernel(
    q_hbm, do_hbm, o_hbm, k_hbm, v_hbm, lse_hbm, pairs_hbm,
    oq_ref, ok_ref, ov_ref,
    kv, qs, dos, do_own, o_own, lse, pairs, dls, dlr, accq, own_g, gsend, grecv, fin_q, fin_kv,
    loc_sem, in_recv, in_send, kvz_recv, kvz_send, kv_recv, kv_send, g_recv, g_send, out_recv, out_send,
):
    s = lax.axis_index("seq")
    h = lax.axis_index("head")

    c_do = pltpu.make_async_copy(do_hbm, do_own, loc_sem.at[0])
    c_o = pltpu.make_async_copy(o_hbm, o_own, loc_sem.at[1])
    c_lse = pltpu.make_async_copy(lse_hbm, lse, loc_sem.at[2])
    c_pairs = pltpu.make_async_copy(pairs_hbm, pairs, loc_sem.at[3])
    for c in (c_do, c_o, c_lse, c_pairs):
        c.start()

    z = s // PLANE
    y = lax.rem(s, PLANE)

    def in_plane(step):
        return z * PLANE + lax.rem(y + step, PLANE)

    up = lax.rem(s + PLANE, PLANE * DEPTH)
    down = lax.rem(s + PLANE * (DEPTH - 1), PLANE * DEPTH)

    above = (z + DEPTH - 1) // DEPTH
    below = (2 * DEPTH - 2 - z) // DEPTH
    barrier = pltpu.get_barrier_semaphore()
    for j in range(1, HEADS):
        pl.semaphore_signal(barrier, inc=1, device_id=(s, lax.rem(h + j, HEADS)), device_id_type=MESH)
    for d in range(1, PLANE):

        @pl.when((d <= y) | (z > 0))
        def _():
            pl.semaphore_signal(
                barrier, inc=1, device_id=(in_plane(PLANE - d), h), device_id_type=MESH
            )

    @pl.when(z > 0)
    def _():
        pl.semaphore_signal(barrier, inc=1, device_id=(down, h), device_id_type=MESH)

    pl.semaphore_wait(barrier, HEADS - 1 + (PLANE - 1 - y) + above * y + below)

    my_rows = pl.ds(pl.multiple_of(h * TOK, TOK), TOK)

    def cols(p, width):
        return pl.ds(pl.multiple_of(p * width, width), width)

    def spread(src, dst, width, n):
        for j in PEER_ORDER:
            p = lax.rem(h + j, HEADS)
            pltpu.make_async_remote_copy(
                src_ref=src.at[:, cols(p, width)],
                dst_ref=dst,
                send_sem=in_send.at[n],
                recv_sem=in_recv.at[0 if n < 2 else n - 1],
                device_id=(s, p),
                device_id_type=MESH,
            ).start()
        pltpu.make_async_copy(
            src.at[:, cols(h, width)], dst, in_recv.at[0 if n < 2 else n - 1]
        ).start()

    spread(k_hbm, kv.at[0, my_rows, 0:D], D, 0)
    spread(v_hbm, kv.at[0, my_rows, D : 2 * D], D, 1)
    spread(q_hbm, qs.at[my_rows, :], 2 * D, 2)
    spread(do_hbm, dos.at[my_rows, :], 2 * D, 3)

    c_do.wait()
    c_o.wait()
    row8 = lax.broadcasted_iota(jnp.int32, (8, 2 * D), 0)
    col8 = lax.broadcasted_iota(jnp.int32, (8, 2 * D), 1)
    select = jnp.where((col8 >= row8 * D) & (col8 < row8 * D + D), 1.0, 0.0).astype(BF16)
    lane = lax.broadcasted_iota(jnp.int32, (8, D), 1)
    low = lax.rem(h, 2) * TOK
    mine = jnp.where((lane >= low) & (lane < low + TOK), 1.0, 0.0)
    for p in range(HEADS):
        c = slice(p * 2 * D, (p + 1) * 2 * D)
        prod = do_own[:, c].astype(F32) * o_own[:, c].astype(F32)
        prod = jnp.concatenate([prod, prod], axis=0)
        hi = prod.astype(BF16)
        mid = (prod - hi.astype(F32)).astype(BF16)
        dls[p] = (dot_nt(select, hi) + dot_nt(select, mid)) * mine
    for j in PEER_ORDER:
        p = lax.rem(h + j, HEADS)
        pltpu.make_async_remote_copy(
            src_ref=dls.at[p],
            dst_ref=dlr.at[h],
            send_sem=in_send.at[4],
            recv_sem=in_recv.at[3],
            device_id=(s, p),
            device_id_type=MESH,
        ).start()
    pltpu.make_async_copy(dls.at[h], dlr.at[h], in_recv.at[3]).start()

    wait_bytes(kv.at[0], in_recv.at[0])

    def kv_in_plane(d, slot, rows, half):
        pltpu.make_async_remote_copy(
            src_ref=kv.at[slot, rows],
            dst_ref=kv.at[d, rows],
            send_sem=kv_send.at[2 * d + half],
            recv_sem=kv_recv.at[2 * d + half],
            device_id=(in_plane(d), h),
            device_id_type=MESH,
        ).start()

    for half in range(2):

        @pl.when(z < DEPTH - 1)
        def _():
            for i in range(half * CHUNKS // 2, (half + 1) * CHUNKS // 2):
                rows = slice(i * CROWS, (i + 1) * CROWS)
                pltpu.make_async_remote_copy(
                    src_ref=kv.at[0, rows],
                    dst_ref=kv.at[4, rows],
                    send_sem=kvz_send.at[i],
                    recv_sem=kvz_recv.at[i],
                    device_id=(up, h),
                    device_id_type=MESH,
                ).start()

        for d in (2, 3, 1):

            @pl.when(y + d < PLANE)
            def _():
                kv_in_plane(d, 0, slice(half * HALF, (half + 1) * HALF), half)

    @pl.when((z > 0) & (y > 0))
    def _():
        for i in range(CHUNKS):
            rows = slice(i * CROWS, (i + 1) * CROWS)
            wait_bytes(kv.at[4, rows], kvz_recv.at[i])
            for d in (2, 3, 1):

                @pl.when(y + d >= PLANE)
                def _():
                    kv_in_plane(d, 4, rows, 2 * i // CHUNKS)

    c_lse.wait()
    c_pairs.wait()
    pa = pairs[0:1, :]
    pc = pairs[1:2, :]
    pm = pairs[2:3, :]
    accq[...] = jnp.zeros_like(accq)

    wait_bytes(qs, in_recv.at[1])
    wait_bytes(dos, in_recv.at[2])
    wait_bytes(dlr, in_recv.at[3])
    delta = jnp.concatenate([dlr[2 * i] + dlr[2 * i + 1] for i in range(HEADS // 2)], axis=1)
    lse2 = lse[...] * LOG2E

    def send_back(d, half):
        rows = pl.ds(pl.multiple_of(half * HALF, HALF), HALF)
        pltpu.make_async_remote_copy(
            src_ref=gsend.at[d, rows],
            dst_ref=grecv.at[d, rows],
            send_sem=g_send.at[2 * d + half],
            recv_sem=g_recv.at[2 * d + half],
            device_id=(in_plane(PLANE - d), h),
            device_id_type=MESH,
        ).start()

    def pair_step(t, carry):
        late = t // 8
        d = late * 4 + (1 - late) * lax.rem(t, 4)
        half = late * lax.rem(t, 4) + (1 - late) * (t // 4)

        @pl.when((z > 0) | (d <= y))
        def _():
            half_pair(d, half)

        return carry

    def half_pair(d, half):
        rows = pl.ds(pl.multiple_of(half * HALF, HALF), HALF)

        @pl.when((d > 0) & (d < 4))
        def _():
            wait_bytes(kv.at[d, rows], kv_recv.at[2 * d + half])

        @pl.when((d == 4) & (y == 0))
        def _():
            for i in range(CHUNKS // 2):
                wait_bytes(kv.at[4, 0:CROWS], kvz_recv.at[half * (CHUNKS // 2) + i])

        match = (pa == s) & (pc == s - d)
        code = jnp.max(jnp.where(match, pm + 1, 0), axis=1, keepdims=True)
        lo = jnp.where((code == 1) | (code == 2), -BLK, jnp.where(code == 3, 0, BLK))
        hi = jnp.where(code == 2, 1, BLK)
        diff = (
            lax.broadcasted_iota(jnp.int32, (HALF, BLK), 0)
            + half * HALF
            - lax.broadcasted_iota(jnp.int32, (HALF, BLK), 1)
        )
        bias = jnp.where((diff > lo) & (diff < hi), 0.0, BIG).astype(F32)
        k = kv[d, rows, 0:D]
        v = kv[d, rows, D : 2 * D]
        kt = k.T
        gk = jnp.zeros((HALF, D), F32)
        gv = jnp.zeros((HALF, D), F32)
        for g in range(2):
            c = slice(g * D, (g + 1) * D)
            q = qs[:, c]
            do = dos[:, c]
            prob = jnp.exp2(dot_nt(k, q) * (SCALE * LOG2E) - lse2[g : g + 1, :] - bias)
            ds = (prob * (dot_nt(v, do) - delta[g : g + 1, :])).astype(BF16)
            gv = gv + dot_nn(prob.astype(BF16), do)
            gk = gk + dot_nn(ds, q)
            accq[c, :] += dot_nn(kt, ds)

        keep = (d == 0) | (d == 4)

        @pl.when(keep)
        def _():
            own_g[d // 4, rows, 0:D] = gk
            own_g[d // 4, rows, D : 2 * D] = gv

        @pl.when(jnp.logical_not(keep))
        def _():
            gsend[d, rows, 0:D] = gk.astype(BF16)
            gsend[d, rows, D : 2 * D] = gv.astype(BF16)

            @pl.when(d > y)
            def _():
                send_back(d, half)

    lax.fori_loop(0, 2 * PLANE, pair_step, 0)
    for half in range(2):
        for d in range(1, PLANE):

            @pl.when(d <= y)
            def _():
                send_back(d, half)

    lax.fori_loop(2 * PLANE, 2 * WIN, pair_step, 0)

    def gather(src, col, width, dst, n, half):
        for j in range(HEADS // 2):
            p = half * (HEADS // 2) + lax.rem(h + j, HEADS // 2)

            @pl.when(p != h)
            def _():
                pltpu.make_async_remote_copy(
                    src_ref=src.at[cols(p, TOK), col],
                    dst_ref=dst.at[:, cols(h, width)],
                    send_sem=out_send.at[n],
                    recv_sem=out_recv.at[n],
                    device_id=(s, p),
                    device_id_type=MESH,
                ).start()

            @pl.when(p == h)
            def _():
                pltpu.make_async_copy(
                    src.at[my_rows, col], dst.at[:, cols(h, width)], out_recv.at[n]
                ).start()

    halves = (slice(0, HALF), slice(HALF, BLK))

    def to_plane_before(i):
        @pl.when(z > 0)
        def _():
            for d in (1, 2, 3):

                @pl.when(y + d >= PLANE)
                def _():
                    wait_bytes(grecv.at[d, halves[i]], g_recv.at[2 * d + i])
                    own_g[1, halves[i]] += grecv[d, halves[i]].astype(F32)

            gsend[0, halves[i]] = own_g[1, halves[i]].astype(BF16)
            pltpu.make_async_remote_copy(
                src_ref=gsend.at[0, halves[i]],
                dst_ref=grecv.at[0, halves[i]],
                send_sem=g_send.at[i],
                recv_sem=g_recv.at[i],
                device_id=(down, h),
                device_id_type=MESH,
            ).start()

    to_plane_before(0)
    for g in range(2):
        c = slice(g * D, (g + 1) * D)
        fin_q[:, c] = (accq[c, :] * SCALE).T.astype(BF16)
    for half in range(2):
        gather(fin_q, slice(0, 2 * D), 2 * D, oq_ref, 0, half)
    to_plane_before(1)

    for i in range(2):
        for d in (1, 2, 3):

            @pl.when(y + d < PLANE)
            def _():
                wait_bytes(grecv.at[d, halves[i]], g_recv.at[2 * d + i])
                own_g[0, halves[i]] += grecv[d, halves[i]].astype(F32)

        @pl.when(z < DEPTH - 1)
        def _():
            wait_bytes(grecv.at[0, halves[i]], g_recv.at[i])
            own_g[0, halves[i]] += grecv[0, halves[i]].astype(F32)

        fin_kv[halves[i], 0:D] = (own_g[0, halves[i], 0:D] * SCALE).astype(BF16)
        fin_kv[halves[i], D : 2 * D] = own_g[0, halves[i], D : 2 * D].astype(BF16)
        gather(fin_kv, slice(0, D), D, ok_ref, 1, i)
        gather(fin_kv, slice(D, 2 * D), D, ov_ref, 2, i)

    most = (HEADS - 1) * TOK
    wait_bytes(kv.at[0, 0:most, 0:D], in_send.at[0])
    wait_bytes(kv.at[0, 0:most, 0:D], in_send.at[1])
    wait_bytes(qs.at[0:most], in_send.at[2])
    wait_bytes(qs.at[0:most], in_send.at[3])
    wait_bytes(dlr.at[0 : HEADS - 1], in_send.at[4])

    @pl.when(z < DEPTH - 1)
    def _():
        for i in range(CHUNKS):
            wait_bytes(kv.at[0, 0:CROWS], kvz_send.at[i])

    for i in range(2):

        @pl.when(z > 0)
        def _():
            wait_bytes(gsend.at[0, halves[i]], g_send.at[i])

        for d in range(1, PLANE):

            @pl.when((y + d < PLANE) | (z > 0))
            def _():
                wait_bytes(kv.at[d, halves[i]], kv_send.at[2 * d + i])

            @pl.when((d <= y) | (z > 0))
            def _():
                wait_bytes(gsend.at[d, halves[i]], g_send.at[2 * d + i])

    wait_bytes(fin_q.at[0:most], out_send.at[0])
    wait_bytes(fin_kv.at[0:most, 0:D], out_send.at[1])
    wait_bytes(fin_kv.at[0:most, 0:D], out_send.at[2])
    wait_bytes(oq_ref, out_recv.at[0])
    wait_bytes(ok_ref, out_recv.at[1])
    wait_bytes(ov_ref, out_recv.at[2])


def hand_on(q_ref, k_ref, v_ref, oq_ref, ok_ref, ov_ref, q_buf, k_buf, v_buf, sem_in, sem_out):
    buffers = ((q_ref, q_buf, oq_ref), (k_ref, k_buf, ok_ref), (v_ref, v_buf, ov_ref))
    arrive = [
        pltpu.make_async_copy(src, buf, sem_in.at[n]) for n, (src, buf, dst) in enumerate(buffers)
    ]
    leave = [
        pltpu.make_async_copy(buf, dst, sem_out.at[n]) for n, (src, buf, dst) in enumerate(buffers)
    ]
    for c in arrive:
        c.start()
    for a, b in zip(arrive, leave):
        a.wait()
        b.start()
    for c in leave:
        c.wait()


def shards(queries, output_gradient, outputs, key_vectors, values, logsum, pair_list):
    any_spec = pl.BlockSpec(memory_space=pl.ANY)
    out_shape = (
        jax.ShapeDtypeStruct((TOK, 2 * D * HEADS), BF16),
        jax.ShapeDtypeStruct((TOK, D * HEADS), BF16),
        jax.ShapeDtypeStruct((TOK, D * HEADS), BF16),
    )
    grads = pl.pallas_call(
        kernel,
        out_shape=out_shape,
        in_specs=[any_spec] * 7,
        out_specs=(any_spec,) * 3,
        scratch_shapes=[
            pltpu.VMEM((WIN, BLK, 2 * D), BF16),
            pltpu.VMEM((BLK, 2 * D), BF16),
            pltpu.VMEM((BLK, 2 * D), BF16),
            pltpu.VMEM((TOK, 2 * D * HEADS), BF16),
            pltpu.VMEM((TOK, 2 * D * HEADS), BF16),
            pltpu.VMEM((2, BLK), F32),
            pltpu.VMEM((3, 500), jnp.int32),
            pltpu.VMEM((HEADS, 8, D), F32),
            pltpu.VMEM((HEADS, 8, D), F32),
            pltpu.VMEM((2 * D, BLK), F32),
            pltpu.VMEM((2, BLK, 2 * D), F32),
            pltpu.VMEM((PLANE, BLK, 2 * D), BF16),
            pltpu.VMEM((PLANE, BLK, 2 * D), BF16),
            pltpu.VMEM((BLK, 2 * D), BF16),
            pltpu.VMEM((BLK, 2 * D), BF16),
            pltpu.SemaphoreType.DMA((4,)),
            pltpu.SemaphoreType.DMA((4,)),
            pltpu.SemaphoreType.DMA((5,)),
            pltpu.SemaphoreType.DMA((CHUNKS,)),
            pltpu.SemaphoreType.DMA((CHUNKS,)),
            pltpu.SemaphoreType.DMA((2 * PLANE,)),
            pltpu.SemaphoreType.DMA((2 * PLANE,)),
            pltpu.SemaphoreType.DMA((2 * PLANE,)),
            pltpu.SemaphoreType.DMA((2 * PLANE,)),
            pltpu.SemaphoreType.DMA((3,)),
            pltpu.SemaphoreType.DMA((3,)),
        ],
        compiler_params=pltpu.CompilerParams(
            collective_id=0, has_side_effects=True, vmem_limit_bytes=60 * 2**20
        ),
        cost_estimate=pl.CostEstimate(
            flops=2 * WIN * 2 * 5 * BLK * BLK * D,
            bytes_accessed=3 * 2**19,
            transcendentals=WIN * 2 * BLK * BLK,
        ),
    )(
        queries, output_gradient, outputs, key_vectors, values, logsum, jnp.transpose(pair_list)
    )
    return pl.pallas_call(
        hand_on,
        out_shape=out_shape,
        in_specs=[any_spec] * 3,
        out_specs=(any_spec,) * 3,
        scratch_shapes=[pltpu.VMEM(o.shape, o.dtype) for o in out_shape]
        + [pltpu.SemaphoreType.DMA((3,)), pltpu.SemaphoreType.DMA((3,))],
        compiler_params=pltpu.CompilerParams(vmem_limit_bytes=60 * 2**20),
    )(*grads)


def solution(mesh):
    tok = P(("seq", "head"), None)
    return jax.shard_map(
        shards,
        mesh=mesh,
        in_specs=(tok, tok, tok, tok, tok, P("head", "seq"), P()),
        out_specs=(tok, tok, tok),
        check_vma=False,
    )
```

```python
import jax
import jax.numpy as jnp
from jax import lax
from jax.experimental import pallas as pl
from jax.experimental.pallas import tpu as pltpu
from jax.sharding import PartitionSpec as P

D = 128
BLK = 512
TOK = 64
HEADS = 8
PLANE = 4
DEPTH = 32
WIN = 5
CHUNKS = 4
CROWS = BLK // CHUNKS
HALF = BLK // 2
LOG2E = 1.4426950408889634
SCALE = 1.0 / D**0.5
BIG = 1e30
F32 = jnp.float32
BF16 = jnp.bfloat16
MESH = pl.DeviceIdType.MESH
PEER_ORDER = (4, 3, 5, 2, 6, 1, 7)


def dot_nt(a, b):
    return lax.dot_general(a, b, (((1,), (1,)), ((), ())), preferred_element_type=F32)


def dot_nn(a, b):
    return lax.dot_general(a, b, (((1,), (0,)), ((), ())), preferred_element_type=F32)


def wait_bytes(ref, sem):
    pltpu.make_async_copy(ref, ref, sem).wait()


def kernel(
    q_hbm, do_hbm, o_hbm, k_hbm, v_hbm, lse_hbm, pairs_hbm,
    oq_ref, ok_ref, ov_ref,
    kv, qs, dos, do_own, o_own, lse, pairs, dls, dlr, accq, own_g, gsend, grecv, fin_q, fin_kv,
    loc_sem, in_recv, in_send, kvz_recv, kvz_send, kv_recv, kv_send, g_recv, g_send, out_recv, out_send,
):
    s = lax.axis_index("seq")
    h = lax.axis_index("head")

    c_do = pltpu.make_async_copy(do_hbm, do_own, loc_sem.at[0])
    c_o = pltpu.make_async_copy(o_hbm, o_own, loc_sem.at[1])
    c_lse = pltpu.make_async_copy(lse_hbm, lse, loc_sem.at[2])
    c_pairs = pltpu.make_async_copy(pairs_hbm, pairs, loc_sem.at[3])
    for c in (c_do, c_o, c_lse, c_pairs):
        c.start()

    z = s // PLANE
    y = lax.rem(s, PLANE)

    def in_plane(step):
        return z * PLANE + lax.rem(y + step, PLANE)

    up = lax.rem(s + PLANE, PLANE * DEPTH)
    down = lax.rem(s + PLANE * (DEPTH - 1), PLANE * DEPTH)

    above = (z + DEPTH - 1) // DEPTH
    below = (2 * DEPTH - 2 - z) // DEPTH
    barrier = pltpu.get_barrier_semaphore()
    for j in range(1, HEADS):
        pl.semaphore_signal(barrier, inc=1, device_id=(s, lax.rem(h + j, HEADS)), device_id_type=MESH)
    for d in range(1, PLANE):

        @pl.when((d <= y) | (z > 0))
        def _():
            pl.semaphore_signal(
                barrier, inc=1, device_id=(in_plane(PLANE - d), h), device_id_type=MESH
            )

    @pl.when(z > 0)
    def _():
        pl.semaphore_signal(barrier, inc=1, device_id=(down, h), device_id_type=MESH)

    pl.semaphore_wait(barrier, HEADS - 1 + (PLANE - 1 - y) + above * y + below)

    my_rows = pl.ds(pl.multiple_of(h * TOK, TOK), TOK)

    def cols(p, width):
        return pl.ds(pl.multiple_of(p * width, width), width)

    def spread(src, dst, width, n):
        for j in PEER_ORDER:
            p = lax.rem(h + j, HEADS)
            pltpu.make_async_remote_copy(
                src_ref=src.at[:, cols(p, width)],
                dst_ref=dst,
                send_sem=in_send.at[n],
                recv_sem=in_recv.at[0 if n < 2 else n - 1],
                device_id=(s, p),
                device_id_type=MESH,
            ).start()
        pltpu.make_async_copy(
            src.at[:, cols(h, width)], dst, in_recv.at[0 if n < 2 else n - 1]
        ).start()

    spread(k_hbm, kv.at[0, my_rows, 0:D], D, 0)
    spread(v_hbm, kv.at[0, my_rows, D : 2 * D], D, 1)
    spread(q_hbm, qs.at[my_rows, :], 2 * D, 2)
    spread(do_hbm, dos.at[my_rows, :], 2 * D, 3)

    c_do.wait()
    c_o.wait()
    row8 = lax.broadcasted_iota(jnp.int32, (8, 2 * D), 0)
    col8 = lax.broadcasted_iota(jnp.int32, (8, 2 * D), 1)
    select = jnp.where((col8 >= row8 * D) & (col8 < row8 * D + D), 1.0, 0.0).astype(BF16)
    lane = lax.broadcasted_iota(jnp.int32, (8, D), 1)
    low = lax.rem(h, 2) * TOK
    mine = jnp.where((lane >= low) & (lane < low + TOK), 1.0, 0.0)
    for p in range(HEADS):
        c = slice(p * 2 * D, (p + 1) * 2 * D)
        prod = do_own[:, c].astype(F32) * o_own[:, c].astype(F32)
        prod = jnp.concatenate([prod, prod], axis=0)
        hi = prod.astype(BF16)
        mid = (prod - hi.astype(F32)).astype(BF16)
        dls[p] = (dot_nt(select, hi) + dot_nt(select, mid)) * mine
    for j in PEER_ORDER:
        p = lax.rem(h + j, HEADS)
        pltpu.make_async_remote_copy(
            src_ref=dls.at[p],
            dst_ref=dlr.at[h],
            send_sem=in_send.at[4],
            recv_sem=in_recv.at[3],
            device_id=(s, p),
            device_id_type=MESH,
        ).start()
    pltpu.make_async_copy(dls.at[h], dlr.at[h], in_recv.at[3]).start()

    wait_bytes(kv.at[0], in_recv.at[0])

    def kv_in_plane(d, slot, rows, half):
        pltpu.make_async_remote_copy(
            src_ref=kv.at[slot, rows],
            dst_ref=kv.at[d, rows],
            send_sem=kv_send.at[2 * d + half],
            recv_sem=kv_recv.at[2 * d + half],
            device_id=(in_plane(d), h),
            device_id_type=MESH,
        ).start()

    for half in range(2):

        @pl.when(z < DEPTH - 1)
        def _():
            for i in range(half * CHUNKS // 2, (half + 1) * CHUNKS // 2):
                rows = slice(i * CROWS, (i + 1) * CROWS)
                pltpu.make_async_remote_copy(
                    src_ref=kv.at[0, rows],
                    dst_ref=kv.at[4, rows],
                    send_sem=kvz_send.at[i],
                    recv_sem=kvz_recv.at[i],
                    device_id=(up, h),
                    device_id_type=MESH,
                ).start()

        for d in (2, 3, 1):

            @pl.when(y + d < PLANE)
            def _():
                kv_in_plane(d, 0, slice(half * HALF, (half + 1) * HALF), half)

    @pl.when((z > 0) & (y > 0))
    def _():
        for i in range(CHUNKS):
            rows = slice(i * CROWS, (i + 1) * CROWS)
            wait_bytes(kv.at[4, rows], kvz_recv.at[i])
            for d in (2, 3, 1):

                @pl.when(y + d >= PLANE)
                def _():
                    kv_in_plane(d, 4, rows, 2 * i // CHUNKS)

    c_lse.wait()
    c_pairs.wait()
    pa = pairs[0:1, :]
    pc = pairs[1:2, :]
    pm = pairs[2:3, :]
    accq[...] = jnp.zeros_like(accq)

    wait_bytes(qs, in_recv.at[1])
    wait_bytes(dos, in_recv.at[2])
    wait_bytes(dlr, in_recv.at[3])
    delta = jnp.concatenate([dlr[2 * i] + dlr[2 * i + 1] for i in range(HEADS // 2)], axis=1)
    lse2 = lse[...] * LOG2E

    def send_back(d, half):
        rows = pl.ds(pl.multiple_of(half * HALF, HALF), HALF)
        pltpu.make_async_remote_copy(
            src_ref=gsend.at[d, rows],
            dst_ref=grecv.at[d, rows],
            send_sem=g_send.at[2 * d + half],
            recv_sem=g_recv.at[2 * d + half],
            device_id=(in_plane(PLANE - d), h),
            device_id_type=MESH,
        ).start()

    def pair_step(t, carry):
        first_row = 1 - (y + 2) // 3
        u = t + first_row * (2 * ((t + 6) // 8) - 8 * (t // 8))
        a = (u + 8) // 10
        b = (u + 6) // 10
        d = 4 * (a - b) + b * (1 + lax.rem(12 + first_row - u, 3))
        half = (1 - a) * u + (a - b) * (u - 2) + b * ((u + 2) // 3 - 2)

        @pl.when((z > 0) | (d <= y))
        def _():
            half_pair(d, half)

        return carry

    def half_pair(d, half):
        rows = pl.ds(pl.multiple_of(half * HALF, HALF), HALF)

        @pl.when((d > 0) & (d < 4))
        def _():
            wait_bytes(kv.at[d, rows], kv_recv.at[2 * d + half])

        @pl.when((d == 4) & (y == 0))
        def _():
            for i in range(CHUNKS // 2):
                wait_bytes(kv.at[4, 0:CROWS], kvz_recv.at[half * (CHUNKS // 2) + i])

        match = (pa == s) & (pc == s - d)
        code = jnp.max(jnp.where(match, pm + 1, 0), axis=1, keepdims=True)
        lo = jnp.where((code == 1) | (code == 2), -BLK, jnp.where(code == 3, 0, BLK))
        hi = jnp.where(code == 2, 1, BLK)
        diff = (
            lax.broadcasted_iota(jnp.int32, (HALF, BLK), 0)
            + half * HALF
            - lax.broadcasted_iota(jnp.int32, (HALF, BLK), 1)
        )
        bias = jnp.where((diff > lo) & (diff < hi), 0.0, BIG).astype(F32)
        k = kv[d, rows, 0:D]
        v = kv[d, rows, D : 2 * D]
        kt = k.T
        gk = jnp.zeros((HALF, D), F32)
        gv = jnp.zeros((HALF, D), F32)
        for g in range(2):
            c = slice(g * D, (g + 1) * D)
            q = qs[:, c]
            do = dos[:, c]
            prob = jnp.exp2(dot_nt(k, q) * (SCALE * LOG2E) - lse2[g : g + 1, :] - bias)
            ds = (prob * (dot_nt(v, do) - delta[g : g + 1, :])).astype(BF16)
            gv = gv + dot_nn(prob.astype(BF16), do)
            gk = gk + dot_nn(ds, q)
            accq[c, :] += dot_nn(kt, ds)

        keep = (d == 0) | (d == 4)

        @pl.when(keep)
        def _():
            own_g[d // 4, rows, 0:D] = gk
            own_g[d // 4, rows, D : 2 * D] = gv

        @pl.when(jnp.logical_not(keep))
        def _():
            gsend[d, rows, 0:D] = gk.astype(BF16)
            gsend[d, rows, D : 2 * D] = gv.astype(BF16)

            @pl.when((d > y) | (z == 0))
            def _():
                send_back(d, half)

    lax.fori_loop(0, 2 * WIN, pair_step, 0)
    for half in range(2):
        for d in range(1, PLANE):

            @pl.when((d <= y) & (z > 0))
            def _():
                send_back(d, half)


    def gather(src, col, width, dst, n, half):
        for j in range(HEADS // 2):
            p = half * (HEADS // 2) + lax.rem(h + j, HEADS // 2)

            @pl.when(p != h)
            def _():
                pltpu.make_async_remote_copy(
                    src_ref=src.at[cols(p, TOK), col],
                    dst_ref=dst.at[:, cols(h, width)],
                    send_sem=out_send.at[n],
                    recv_sem=out_recv.at[n],
                    device_id=(s, p),
                    device_id_type=MESH,
                ).start()

            @pl.when(p == h)
            def _():
                pltpu.make_async_copy(
                    src.at[my_rows, col], dst.at[:, cols(h, width)], out_recv.at[n]
                ).start()

    halves = (slice(0, HALF), slice(HALF, BLK))

    def to_plane_before(i):
        @pl.when(z > 0)
        def _():
            for d in (1, 2, 3):

                @pl.when(y + d >= PLANE)
                def _():
                    wait_bytes(grecv.at[d, halves[i]], g_recv.at[2 * d + i])
                    own_g[1, halves[i]] += grecv[d, halves[i]].astype(F32)

            gsend[0, halves[i]] = own_g[1, halves[i]].astype(BF16)
            pltpu.make_async_remote_copy(
                src_ref=gsend.at[0, halves[i]],
                dst_ref=grecv.at[0, halves[i]],
                send_sem=g_send.at[i],
                recv_sem=g_recv.at[i],
                device_id=(down, h),
                device_id_type=MESH,
            ).start()

    to_plane_before(0)
    for g in range(2):
        c = slice(g * D, (g + 1) * D)
        fin_q[:, c] = (accq[c, :] * SCALE).T.astype(BF16)
    for half in range(2):
        gather(fin_q, slice(0, 2 * D), 2 * D, oq_ref, 0, half)
    to_plane_before(1)

    for i in range(2):
        for d in (1, 2, 3):

            @pl.when(y + d < PLANE)
            def _():
                wait_bytes(grecv.at[d, halves[i]], g_recv.at[2 * d + i])
                own_g[0, halves[i]] += grecv[d, halves[i]].astype(F32)

        @pl.when(z < DEPTH - 1)
        def _():
            wait_bytes(grecv.at[0, halves[i]], g_recv.at[i])
            own_g[0, halves[i]] += grecv[0, halves[i]].astype(F32)

        fin_kv[halves[i], 0:D] = (own_g[0, halves[i], 0:D] * SCALE).astype(BF16)
        fin_kv[halves[i], D : 2 * D] = own_g[0, halves[i], D : 2 * D].astype(BF16)
        gather(fin_kv, slice(0, D), D, ok_ref, 1, i)
        gather(fin_kv, slice(D, 2 * D), D, ov_ref, 2, i)

    most = (HEADS - 1) * TOK
    wait_bytes(kv.at[0, 0:most, 0:D], in_send.at[0])
    wait_bytes(kv.at[0, 0:most, 0:D], in_send.at[1])
    wait_bytes(qs.at[0:most], in_send.at[2])
    wait_bytes(qs.at[0:most], in_send.at[3])
    wait_bytes(dlr.at[0 : HEADS - 1], in_send.at[4])

    @pl.when(z < DEPTH - 1)
    def _():
        for i in range(CHUNKS):
            wait_bytes(kv.at[0, 0:CROWS], kvz_send.at[i])

    for i in range(2):

        @pl.when(z > 0)
        def _():
            wait_bytes(gsend.at[0, halves[i]], g_send.at[i])

        for d in range(1, PLANE):

            @pl.when((y + d < PLANE) | (z > 0))
            def _():
                wait_bytes(kv.at[d, halves[i]], kv_send.at[2 * d + i])

            @pl.when((d <= y) | (z > 0))
            def _():
                wait_bytes(gsend.at[d, halves[i]], g_send.at[2 * d + i])

    wait_bytes(fin_q.at[0:most], out_send.at[0])
    wait_bytes(fin_kv.at[0:most, 0:D], out_send.at[1])
    wait_bytes(fin_kv.at[0:most, 0:D], out_send.at[2])
    wait_bytes(oq_ref, out_recv.at[0])
    wait_bytes(ok_ref, out_recv.at[1])
    wait_bytes(ov_ref, out_recv.at[2])


def hand_on(q_ref, k_ref, v_ref, oq_ref, ok_ref, ov_ref, q_buf, k_buf, v_buf, sem_in, sem_out):
    buffers = ((q_ref, q_buf, oq_ref), (k_ref, k_buf, ok_ref), (v_ref, v_buf, ov_ref))
    arrive = [
        pltpu.make_async_copy(src, buf, sem_in.at[n]) for n, (src, buf, dst) in enumerate(buffers)
    ]
    leave = [
        pltpu.make_async_copy(buf, dst, sem_out.at[n]) for n, (src, buf, dst) in enumerate(buffers)
    ]
    for c in arrive:
        c.start()
    for a, b in zip(arrive, leave):
        a.wait()
        b.start()
    for c in leave:
        c.wait()


def shards(queries, output_gradient, outputs, key_vectors, values, logsum, pair_list):
    any_spec = pl.BlockSpec(memory_space=pl.ANY)
    out_shape = (
        jax.ShapeDtypeStruct((TOK, 2 * D * HEADS), BF16),
        jax.ShapeDtypeStruct((TOK, D * HEADS), BF16),
        jax.ShapeDtypeStruct((TOK, D * HEADS), BF16),
    )
    grads = pl.pallas_call(
        kernel,
        out_shape=out_shape,
        in_specs=[any_spec] * 7,
        out_specs=(any_spec,) * 3,
        scratch_shapes=[
            pltpu.VMEM((WIN, BLK, 2 * D), BF16),
            pltpu.VMEM((BLK, 2 * D), BF16),
            pltpu.VMEM((BLK, 2 * D), BF16),
            pltpu.VMEM((TOK, 2 * D * HEADS), BF16),
            pltpu.VMEM((TOK, 2 * D * HEADS), BF16),
            pltpu.VMEM((2, BLK), F32),
            pltpu.VMEM((3, 500), jnp.int32),
            pltpu.VMEM((HEADS, 8, D), F32),
            pltpu.VMEM((HEADS, 8, D), F32),
            pltpu.VMEM((2 * D, BLK), F32),
            pltpu.VMEM((2, BLK, 2 * D), F32),
            pltpu.VMEM((PLANE, BLK, 2 * D), BF16),
            pltpu.VMEM((PLANE, BLK, 2 * D), BF16),
            pltpu.VMEM((BLK, 2 * D), BF16),
            pltpu.VMEM((BLK, 2 * D), BF16),
            pltpu.SemaphoreType.DMA((4,)),
            pltpu.SemaphoreType.DMA((4,)),
            pltpu.SemaphoreType.DMA((5,)),
            pltpu.SemaphoreType.DMA((CHUNKS,)),
            pltpu.SemaphoreType.DMA((CHUNKS,)),
            pltpu.SemaphoreType.DMA((2 * PLANE,)),
            pltpu.SemaphoreType.DMA((2 * PLANE,)),
            pltpu.SemaphoreType.DMA((2 * PLANE,)),
            pltpu.SemaphoreType.DMA((2 * PLANE,)),
            pltpu.SemaphoreType.DMA((3,)),
            pltpu.SemaphoreType.DMA((3,)),
        ],
        compiler_params=pltpu.CompilerParams(
            collective_id=0, has_side_effects=True, vmem_limit_bytes=60 * 2**20
        ),
        cost_estimate=pl.CostEstimate(
            flops=2 * WIN * 2 * 5 * BLK * BLK * D,
            bytes_accessed=3 * 2**19,
            transcendentals=WIN * 2 * BLK * BLK,
        ),
    )(
        queries, output_gradient, outputs, key_vectors, values, logsum, jnp.transpose(pair_list)
    )
    return pl.pallas_call(
        hand_on,
        out_shape=out_shape,
        in_specs=[any_spec] * 3,
        out_specs=(any_spec,) * 3,
        scratch_shapes=[pltpu.VMEM(o.shape, o.dtype) for o in out_shape]
        + [pltpu.SemaphoreType.DMA((3,)), pltpu.SemaphoreType.DMA((3,))],
        compiler_params=pltpu.CompilerParams(vmem_limit_bytes=60 * 2**20),
    )(*grads)


def solution(mesh):
    tok = P(("seq", "head"), None)
    return jax.shard_map(
        shards,
        mesh=mesh,
        in_specs=(tok, tok, tok, tok, tok, P("head", "seq"), P()),
        out_specs=(tok, tok, tok),
        check_vma=False,
    )
```

```python
import jax
import jax.numpy as jnp
from jax import lax
from jax.experimental import pallas as pl
from jax.experimental.pallas import tpu as pltpu
from jax.sharding import PartitionSpec as P

D = 128
BLK = 512
TOK = 64
HEADS = 8
PLANE = 4
DEPTH = 32
WIN = 5
CHUNKS = 4
CROWS = BLK // CHUNKS
HALF = BLK // 2
LOG2E = 1.4426950408889634
SCALE = 1.0 / D**0.5
BIG = 1e30
F32 = jnp.float32
BF16 = jnp.bfloat16
MESH = pl.DeviceIdType.MESH
PEER_ORDER = (4, 3, 5, 2, 6, 1, 7)


def dot_nt(a, b):
    return lax.dot_general(a, b, (((1,), (1,)), ((), ())), preferred_element_type=F32)


def dot_nn(a, b):
    return lax.dot_general(a, b, (((1,), (0,)), ((), ())), preferred_element_type=F32)


def wait_bytes(ref, sem):
    pltpu.make_async_copy(ref, ref, sem).wait()


def kernel(
    q_hbm, do_hbm, o_hbm, k_hbm, v_hbm, lse_hbm, pairs_hbm,
    oq_ref, ok_ref, ov_ref,
    kv, qs, dos, do_own, o_own, lse, pairs, dls, dlr, accq, own_g, gsend, grecv, fin_q, fin_kv,
    loc_sem, in_recv, in_send, kvz_recv, kvz_send, kv_recv, kv_send, g_recv, g_send, out_recv, out_send,
):
    s = lax.axis_index("seq")
    h = lax.axis_index("head")

    c_do = pltpu.make_async_copy(do_hbm, do_own, loc_sem.at[0])
    c_o = pltpu.make_async_copy(o_hbm, o_own, loc_sem.at[1])
    c_lse = pltpu.make_async_copy(lse_hbm, lse, loc_sem.at[2])
    c_pairs = pltpu.make_async_copy(pairs_hbm, pairs, loc_sem.at[3])
    for c in (c_do, c_o, c_lse, c_pairs):
        c.start()

    z = s // PLANE
    y = lax.rem(s, PLANE)

    def in_plane(step):
        return z * PLANE + lax.rem(y + step, PLANE)

    up = lax.rem(s + PLANE, PLANE * DEPTH)
    down = lax.rem(s + PLANE * (DEPTH - 1), PLANE * DEPTH)

    above = (z + DEPTH - 1) // DEPTH
    below = (2 * DEPTH - 2 - z) // DEPTH
    barrier = pltpu.get_barrier_semaphore()
    for j in range(1, HEADS):
        pl.semaphore_signal(barrier, inc=1, device_id=(s, lax.rem(h + j, HEADS)), device_id_type=MESH)
    for d in range(1, PLANE):

        @pl.when((d <= y) | (z > 0))
        def _():
            pl.semaphore_signal(
                barrier, inc=1, device_id=(in_plane(PLANE - d), h), device_id_type=MESH
            )

    @pl.when(z > 0)
    def _():
        pl.semaphore_signal(barrier, inc=1, device_id=(down, h), device_id_type=MESH)

    pl.semaphore_wait(barrier, HEADS - 1 + (PLANE - 1 - y) + above * y + below)

    my_rows = pl.ds(pl.multiple_of(h * TOK, TOK), TOK)

    def cols(p, width):
        return pl.ds(pl.multiple_of(p * width, width), width)

    def spread(src, dst, width, n):
        for j in PEER_ORDER:
            p = lax.rem(h + j, HEADS)
            pltpu.make_async_remote_copy(
                src_ref=src.at[:, cols(p, width)],
                dst_ref=dst,
                send_sem=in_send.at[n],
                recv_sem=in_recv.at[0 if n < 2 else n - 1],
                device_id=(s, p),
                device_id_type=MESH,
            ).start()
        pltpu.make_async_copy(
            src.at[:, cols(h, width)], dst, in_recv.at[0 if n < 2 else n - 1]
        ).start()

    spread(k_hbm, kv.at[0, my_rows, 0:D], D, 0)
    spread(v_hbm, kv.at[0, my_rows, D : 2 * D], D, 1)
    spread(q_hbm, qs.at[my_rows, :], 2 * D, 2)
    spread(do_hbm, dos.at[my_rows, :], 2 * D, 3)

    c_do.wait()
    c_o.wait()
    row8 = lax.broadcasted_iota(jnp.int32, (8, 2 * D), 0)
    col8 = lax.broadcasted_iota(jnp.int32, (8, 2 * D), 1)
    select = jnp.where((col8 >= row8 * D) & (col8 < row8 * D + D), 1.0, 0.0).astype(BF16)
    lane = lax.broadcasted_iota(jnp.int32, (8, D), 1)
    low = lax.rem(h, 2) * TOK
    mine = jnp.where((lane >= low) & (lane < low + TOK), 1.0, 0.0)
    for p in range(HEADS):
        c = slice(p * 2 * D, (p + 1) * 2 * D)
        prod = do_own[:, c].astype(F32) * o_own[:, c].astype(F32)
        prod = jnp.concatenate([prod, prod], axis=0)
        hi = prod.astype(BF16)
        mid = (prod - hi.astype(F32)).astype(BF16)
        dls[p] = (dot_nt(select, hi) + dot_nt(select, mid)) * mine
    for j in PEER_ORDER:
        p = lax.rem(h + j, HEADS)
        pltpu.make_async_remote_copy(
            src_ref=dls.at[p],
            dst_ref=dlr.at[h],
            send_sem=in_send.at[4],
            recv_sem=in_recv.at[3],
            device_id=(s, p),
            device_id_type=MESH,
        ).start()
    pltpu.make_async_copy(dls.at[h], dlr.at[h], in_recv.at[3]).start()

    wait_bytes(kv.at[0], in_recv.at[0])

    def kv_in_plane(d, slot, rows, half):
        pltpu.make_async_remote_copy(
            src_ref=kv.at[slot, rows],
            dst_ref=kv.at[d, rows],
            send_sem=kv_send.at[2 * d + half],
            recv_sem=kv_recv.at[2 * d + half],
            device_id=(in_plane(d), h),
            device_id_type=MESH,
        ).start()

    for half in range(2):

        @pl.when(z < DEPTH - 1)
        def _():
            for i in range(half * CHUNKS // 2, (half + 1) * CHUNKS // 2):
                rows = slice(i * CROWS, (i + 1) * CROWS)
                pltpu.make_async_remote_copy(
                    src_ref=kv.at[0, rows],
                    dst_ref=kv.at[4, rows],
                    send_sem=kvz_send.at[i],
                    recv_sem=kvz_recv.at[i],
                    device_id=(up, h),
                    device_id_type=MESH,
                ).start()

        for d in (2, 3, 1):

            @pl.when(y + d < PLANE)
            def _():
                kv_in_plane(d, 0, slice(half * HALF, (half + 1) * HALF), half)

    @pl.when((z > 0) & (y > 0))
    def _():
        for i in range(CHUNKS):
            rows = slice(i * CROWS, (i + 1) * CROWS)
            wait_bytes(kv.at[4, rows], kvz_recv.at[i])
            for d in (2, 3, 1):

                @pl.when(y + d >= PLANE)
                def _():
                    kv_in_plane(d, 4, rows, 2 * i // CHUNKS)

    c_lse.wait()
    c_pairs.wait()
    pa = pairs[0:1, :]
    pc = pairs[1:2, :]
    pm = pairs[2:3, :]
    accq[...] = jnp.zeros_like(accq)

    wait_bytes(qs, in_recv.at[1])
    wait_bytes(dos, in_recv.at[2])
    wait_bytes(dlr, in_recv.at[3])
    delta = jnp.concatenate([dlr[2 * i] + dlr[2 * i + 1] for i in range(HEADS // 2)], axis=1)
    lse2 = lse[...] * LOG2E

    def send_back(d, half):
        rows = pl.ds(pl.multiple_of(half * HALF, HALF), HALF)
        pltpu.make_async_remote_copy(
            src_ref=gsend.at[d, rows],
            dst_ref=grecv.at[d, rows],
            send_sem=g_send.at[2 * d + half],
            recv_sem=g_recv.at[2 * d + half],
            device_id=(in_plane(PLANE - d), h),
            device_id_type=MESH,
        ).start()

    def pair_step(t, carry):
        first_row = 1 - (y + 2) // 3
        u = t + first_row * (2 * ((t + 6) // 8) - 8 * (t // 8))
        a = (u + 8) // 10
        b = (u + 6) // 10
        d = 4 * (a - b) + b * (1 + lax.rem(12 + first_row - u, 3))
        half = (1 - a) * u + (a - b) * (u - 2) + b * ((u + 2) // 3 - 2)

        @pl.when((z > 0) | (d <= y))
        def _():
            half_pair(d, half)

        return carry

    def half_pair(d, half):
        rows = pl.ds(pl.multiple_of(half * HALF, HALF), HALF)

        @pl.when((d > 0) & (d < 4))
        def _():
            wait_bytes(kv.at[d, rows], kv_recv.at[2 * d + half])

        @pl.when((d == 4) & (y == 0))
        def _():
            for i in range(CHUNKS // 2):
                wait_bytes(kv.at[4, 0:CROWS], kvz_recv.at[half * (CHUNKS // 2) + i])

        match = (pa == s) & (pc == s - d)
        code = jnp.max(jnp.where(match, pm + 1, 0), axis=1, keepdims=True)
        lo = jnp.where((code == 1) | (code == 2), -BLK, jnp.where(code == 3, 0, BLK))
        hi = jnp.where(code == 2, 1, BLK)
        diff = (
            lax.broadcasted_iota(jnp.int32, (HALF, BLK), 0)
            + half * HALF
            - lax.broadcasted_iota(jnp.int32, (HALF, BLK), 1)
        )
        bias = jnp.where((diff > lo) & (diff < hi), 0.0, BIG).astype(F32)
        k = kv[d, rows, 0:D]
        v = kv[d, rows, D : 2 * D]
        kt = k.T
        gk = jnp.zeros((HALF, D), F32)
        gv = jnp.zeros((HALF, D), F32)
        for g in range(2):
            c = slice(g * D, (g + 1) * D)
            q = qs[:, c]
            do = dos[:, c]
            prob = jnp.exp2(dot_nt(k, q) * (SCALE * LOG2E) - lse2[g : g + 1, :] - bias)
            ds = (prob * (dot_nt(v, do) - delta[g : g + 1, :])).astype(BF16)
            gv = gv + dot_nn(prob.astype(BF16), do)
            gk = gk + dot_nn(ds, q)
            accq[c, :] += dot_nn(kt, ds)

        keep = (d == 0) | (d == 4)

        @pl.when(keep)
        def _():
            own_g[d // 4, rows, 0:D] = gk
            own_g[d // 4, rows, D : 2 * D] = gv

        @pl.when(jnp.logical_not(keep))
        def _():
            gsend[d, rows, 0:D] = gk.astype(BF16)
            gsend[d, rows, D : 2 * D] = gv.astype(BF16)

            @pl.when((d > y) | (z == 0))
            def _():
                send_back(d, half)

    lax.fori_loop(0, 2 * WIN, pair_step, 0)
    for half in range(2):
        for d in range(1, PLANE):

            @pl.when((d <= y) & (z > 0))
            def _():
                send_back(d, half)


    def gather(src, col, width, dst, n, first, count):
        for j in range(count):
            p = first + lax.rem(h + j, count)

            @pl.when(p != h)
            def _():
                pltpu.make_async_remote_copy(
                    src_ref=src.at[cols(p, TOK), col],
                    dst_ref=dst.at[:, cols(h, width)],
                    send_sem=out_send.at[n],
                    recv_sem=out_recv.at[n],
                    device_id=(s, p),
                    device_id_type=MESH,
                ).start()

            @pl.when(p == h)
            def _():
                pltpu.make_async_copy(
                    src.at[my_rows, col], dst.at[:, cols(h, width)], out_recv.at[n]
                ).start()

    halves = (slice(0, HALF), slice(HALF, BLK))
    middle = HALF + HALF // 2
    pieces = (((0, HALF, 0),), ((HALF, middle, 1), (middle, BLK, 2 * PLANE)))

    def to_plane_before(i):
        @pl.when(z > 0)
        def _():
            for d in (1, 2, 3):

                @pl.when(y + d >= PLANE)
                def _():
                    wait_bytes(grecv.at[d, halves[i]], g_recv.at[2 * d + i])
                    own_g[1, halves[i]] += grecv[d, halves[i]].astype(F32)

            for low_row, end, n in pieces[i]:
                rows = slice(low_row, end)
                gsend[0, rows] = own_g[1, rows].astype(BF16)
                pltpu.make_async_remote_copy(
                    src_ref=gsend.at[0, rows],
                    dst_ref=grecv.at[0, rows],
                    send_sem=g_send.at[n],
                    recv_sem=g_recv.at[n],
                    device_id=(down, h),
                    device_id_type=MESH,
                ).start()

    to_plane_before(0)
    for g in range(2):
        c = slice(g * D, (g + 1) * D)
        fin_q[:, c] = (accq[c, :] * SCALE).T.astype(BF16)
    for half in range(2):
        gather(fin_q, slice(0, 2 * D), 2 * D, oq_ref, 0, half * (HEADS // 2), HEADS // 2)
    to_plane_before(1)

    for i in range(2):
        for d in (1, 2, 3):

            @pl.when(y + d < PLANE)
            def _():
                wait_bytes(grecv.at[d, halves[i]], g_recv.at[2 * d + i])
                own_g[0, halves[i]] += grecv[d, halves[i]].astype(F32)

        for low_row, end, n in pieces[i]:
            rows = slice(low_row, end)

            @pl.when(z < DEPTH - 1)
            def _():
                wait_bytes(grecv.at[0, rows], g_recv.at[n])
                own_g[0, rows] += grecv[0, rows].astype(F32)

            fin_kv[rows, 0:D] = (own_g[0, rows, 0:D] * SCALE).astype(BF16)
            fin_kv[rows, D : 2 * D] = own_g[0, rows, D : 2 * D].astype(BF16)
            peers = (low_row // TOK, (end - low_row) // TOK)
            gather(fin_kv, slice(0, D), D, ok_ref, 1, *peers)
            gather(fin_kv, slice(D, 2 * D), D, ov_ref, 2, *peers)

    most = (HEADS - 1) * TOK
    wait_bytes(kv.at[0, 0:most, 0:D], in_send.at[0])
    wait_bytes(kv.at[0, 0:most, 0:D], in_send.at[1])
    wait_bytes(qs.at[0:most], in_send.at[2])
    wait_bytes(qs.at[0:most], in_send.at[3])
    wait_bytes(dlr.at[0 : HEADS - 1], in_send.at[4])

    @pl.when(z < DEPTH - 1)
    def _():
        for i in range(CHUNKS):
            wait_bytes(kv.at[0, 0:CROWS], kvz_send.at[i])

    for i in range(2):

        @pl.when(z > 0)
        def _():
            for low_row, end, n in pieces[i]:
                wait_bytes(gsend.at[0, low_row:end], g_send.at[n])

        for d in range(1, PLANE):

            @pl.when((y + d < PLANE) | (z > 0))
            def _():
                wait_bytes(kv.at[d, halves[i]], kv_send.at[2 * d + i])

            @pl.when((d <= y) | (z > 0))
            def _():
                wait_bytes(gsend.at[d, halves[i]], g_send.at[2 * d + i])

    wait_bytes(fin_q.at[0:most], out_send.at[0])
    wait_bytes(fin_kv.at[0:most, 0:D], out_send.at[1])
    wait_bytes(fin_kv.at[0:most, 0:D], out_send.at[2])
    wait_bytes(oq_ref, out_recv.at[0])
    wait_bytes(ok_ref, out_recv.at[1])
    wait_bytes(ov_ref, out_recv.at[2])


def hand_on(q_ref, k_ref, v_ref, oq_ref, ok_ref, ov_ref, q_buf, k_buf, v_buf, sem_in, sem_out):
    buffers = ((q_ref, q_buf, oq_ref), (k_ref, k_buf, ok_ref), (v_ref, v_buf, ov_ref))
    arrive = [
        pltpu.make_async_copy(src, buf, sem_in.at[n]) for n, (src, buf, dst) in enumerate(buffers)
    ]
    leave = [
        pltpu.make_async_copy(buf, dst, sem_out.at[n]) for n, (src, buf, dst) in enumerate(buffers)
    ]
    for c in arrive:
        c.start()
    for a, b in zip(arrive, leave):
        a.wait()
        b.start()
    for c in leave:
        c.wait()


def shards(queries, output_gradient, outputs, key_vectors, values, logsum, pair_list):
    any_spec = pl.BlockSpec(memory_space=pl.ANY)
    out_shape = (
        jax.ShapeDtypeStruct((TOK, 2 * D * HEADS), BF16),
        jax.ShapeDtypeStruct((TOK, D * HEADS), BF16),
        jax.ShapeDtypeStruct((TOK, D * HEADS), BF16),
    )
    grads = pl.pallas_call(
        kernel,
        out_shape=out_shape,
        in_specs=[any_spec] * 7,
        out_specs=(any_spec,) * 3,
        scratch_shapes=[
            pltpu.VMEM((WIN, BLK, 2 * D), BF16),
            pltpu.VMEM((BLK, 2 * D), BF16),
            pltpu.VMEM((BLK, 2 * D), BF16),
            pltpu.VMEM((TOK, 2 * D * HEADS), BF16),
            pltpu.VMEM((TOK, 2 * D * HEADS), BF16),
            pltpu.VMEM((2, BLK), F32),
            pltpu.VMEM((3, 500), jnp.int32),
            pltpu.VMEM((HEADS, 8, D), F32),
            pltpu.VMEM((HEADS, 8, D), F32),
            pltpu.VMEM((2 * D, BLK), F32),
            pltpu.VMEM((2, BLK, 2 * D), F32),
            pltpu.VMEM((PLANE, BLK, 2 * D), BF16),
            pltpu.VMEM((PLANE, BLK, 2 * D), BF16),
            pltpu.VMEM((BLK, 2 * D), BF16),
            pltpu.VMEM((BLK, 2 * D), BF16),
            pltpu.SemaphoreType.DMA((4,)),
            pltpu.SemaphoreType.DMA((4,)),
            pltpu.SemaphoreType.DMA((5,)),
            pltpu.SemaphoreType.DMA((CHUNKS,)),
            pltpu.SemaphoreType.DMA((CHUNKS,)),
            pltpu.SemaphoreType.DMA((2 * PLANE,)),
            pltpu.SemaphoreType.DMA((2 * PLANE,)),
            pltpu.SemaphoreType.DMA((2 * PLANE + 1,)),
            pltpu.SemaphoreType.DMA((2 * PLANE + 1,)),
            pltpu.SemaphoreType.DMA((3,)),
            pltpu.SemaphoreType.DMA((3,)),
        ],
        compiler_params=pltpu.CompilerParams(
            collective_id=0, has_side_effects=True, vmem_limit_bytes=60 * 2**20
        ),
        cost_estimate=pl.CostEstimate(
            flops=2 * WIN * 2 * 5 * BLK * BLK * D,
            bytes_accessed=3 * 2**19,
            transcendentals=WIN * 2 * BLK * BLK,
        ),
    )(
        queries, output_gradient, outputs, key_vectors, values, logsum, jnp.transpose(pair_list)
    )
    return pl.pallas_call(
        hand_on,
        out_shape=out_shape,
        in_specs=[any_spec] * 3,
        out_specs=(any_spec,) * 3,
        scratch_shapes=[pltpu.VMEM(o.shape, o.dtype) for o in out_shape]
        + [pltpu.SemaphoreType.DMA((3,)), pltpu.SemaphoreType.DMA((3,))],
        compiler_params=pltpu.CompilerParams(vmem_limit_bytes=60 * 2**20),
    )(*grads)


def solution(mesh):
    tok = P(("seq", "head"), None)
    return jax.shard_map(
        shards,
        mesh=mesh,
        in_specs=(tok, tok, tok, tok, tok, P("head", "seq"), P()),
        out_specs=(tok, tok, tok),
        check_vma=False,
    )
```
